256 devices in a mesh: blk: 128 (over z, x, y), rep: 2 (over core).
Axes of the slice: x: 4, y: 4, z: 8, core: 2. Of those that a mesh axis runs over, the one named last changes fastest.
Arguments:
- points: bfloat16 [4096, 1024], P('blk', 'rep'), may hold values from -16 to 16
- centroids: float32 [131072, 1024], P('blk', 'rep'), may hold values from -0.15 to 0.15
Outputs:
- new_centroids: float32 [131072, 1024], P('blk', 'rep')
- cluster_mass: float32 [131072], P('blk')
The draws below stay inside these ranges and needn't reach their ends.
All inputs are finite; a program needn't handle non-finite values.
Results may differ from the reference program's by a relative error of at most 0.0065.
Values may be sent and summed in bfloat16 or wider, within the bound.
A program may use at most 128 MiB of HBM per device.

```python
import math
import jax
import jax.numpy as jnp
from jax import lax

D = 1024
K_DEV = 1024
ITERS = 3
TOKENS = 4096
K = 131072


def centroid_base(key):
    base = jax.random.normal(key, (K, D), jnp.float32) * D ** (-0.5)
    base = jnp.clip(base, -0.15, 0.15)
    return base


def draw_centroids(key, part):
    base = centroid_base(key)
    return base.astype(jnp.float32)


def draw_points(key, part):
    key = jax.random.fold_in(key, 5)
    values = jnp.clip(jax.random.normal(key, (TOKENS, D), jnp.float32), -6.0, 6.0)
    return jnp.clip(values, -16.0, 16.0).astype(jnp.bfloat16)


def setup_inputs(seed: int = 0) -> dict:
    seeds = jax.random.split(jax.random.key(seed), 3)
    points = draw_points(jax.random.fold_in(seeds[2], 71), 0)
    centroids = draw_centroids(jax.random.fold_in(seeds[2], 71), 0)
    return dict(points=points, centroids=centroids)


SCALE = 3.0


def reference(points, centroids):
    npts = points.shape[0]
    ncent = centroids.shape[0]
    nblocks = ncent // K_DEV
    centroid_bf = centroids.astype(jnp.bfloat16).reshape(nblocks, K_DEV, D)
    exact = centroids.reshape(nblocks, K_DEV, D)
    log_points = math.log(npts)
    log_cents = math.log(ncent)
    prior = npts / ncent
    point_pot = jnp.zeros((npts,), jnp.float32)
    cluster_pot = jnp.zeros((nblocks, K_DEV), jnp.float32)
    for sweep in range(ITERS):
        def block_step(carry, block):
            row_peak, row_mass = carry
            logits = SCALE * jnp.dot(points, block.T, preferred_element_type=jnp.float32)
            shifted = logits + point_pot[:, None]
            col_peak = jnp.max(shifted, axis=0)
            col_sum = jnp.sum(jnp.exp(shifted - col_peak[None, :]), axis=0)
            pot = -log_cents - (col_peak + jnp.log(col_sum))
            moved = logits + pot[None, :]
            block_peak = jnp.max(moved, axis=1)
            top_value = jnp.maximum(row_peak, block_peak)
            row_mass = row_mass * jnp.exp(row_peak - top_value) + jnp.sum(jnp.exp(moved - top_value[:, None]), axis=1)
            return (top_value, row_mass), pot

        start = (jnp.full((npts,), -jnp.inf, jnp.float32), jnp.zeros((npts,), jnp.float32))
        (row_peak, row_mass), cluster_pot = lax.scan(block_step, start, centroid_bf)
        point_pot = -log_points - (row_peak + jnp.log(row_mass))

    def final_step(carry, inputs):
        block, pot, old = inputs
        logits = SCALE * jnp.dot(points, block.T, preferred_element_type=jnp.float32)
        plan = jnp.exp(logits + point_pot[:, None] + pot[None, :] + log_points)
        mass = jnp.sum(plan, axis=0)
        weights = plan.astype(jnp.bfloat16)
        numerator = jnp.dot(weights.T, points, preferred_element_type=jnp.float32)
        fresh = (numerator + prior * old) / (mass + prior)[:, None]
        return carry, (fresh, mass)

    _, (fresh, mass) = lax.scan(final_step, 0, (centroid_bf, cluster_pot, exact))
    return fresh.reshape(ncent, D), mass.reshape(ncent)
```

```python
import math
from functools import reduce

import jax
import jax.numpy as jnp
from jax import lax
from jax.experimental import pallas as pl
from jax.experimental.pallas import tpu as pltpu
from jax.sharding import PartitionSpec as P

ITERS = 3
SCALE = 3.0
NZ, NX, NY = 8, 4, 4
CENTS = 1024
HALF = 512
ROWS = 16
PTS = NZ * NX * NY * ROWS
TILES = 8
LANES = 128
PBLOCKS = PTS // LANES
CGROUPS = CENTS // 8
LOG2_POINTS = 12.0
LOG2_CENTS = 17.0
PRIOR = 4096 / 131072
MESH = pl.DeviceIdType.MESH
GATHER_SEMS = 72
STAGE_SEMS = 14
STAGES = ((0, NY), (NY - 1, NX), (NY + NX - 2, NZ))


def kernel(points_ref, cent_ref, out_ref, mass_ref, pts, swap, cbf, logits, weights, col_max, col_sum,
           cpot, rpot, csend, crecv, rsend, rrecv, msend, mrecv, nsend, nrecv,
           gs, gr, its, itr, fs, fr):
    blk = lax.axis_index("blk")
    core = lax.axis_index("rep")
    other = 1 - core
    z = lax.div(blk, NX * NY)
    x = lax.rem(lax.div(blk, NY), NX)
    y = lax.rem(blk, NY)

    def on_z(i):
        return (lax.rem(i, NZ) * (NX * NY) + x * NY + y, core)

    def on_x(i):
        return (z * (NX * NY) + lax.rem(i, NX) * NY + y, core)

    def on_y(i):
        return (z * (NX * NY) + x * NY + lax.rem(i, NY), core)

    sibling = (blk, other)

    barrier = pltpu.get_barrier_semaphore()
    pl.semaphore_signal(barrier, inc=1, device_id=sibling, device_id_type=MESH)
    for pos, n, at in ((y, NY, on_y), (x, NX, on_x), (z, NZ, on_z)):
        for d in range(1, n):
            pl.semaphore_signal(barrier, inc=1, device_id=at(pos + d), device_id_type=MESH)
    pl.semaphore_wait(barrier, NZ + NX + NY - 2)

    pending = []
    count = [0]

    def remote(src, dst, send_sem, recv_sem, device):
        copy = pltpu.make_async_remote_copy(
            src_ref=src, dst_ref=dst, send_sem=send_sem, recv_sem=recv_sem,
            device_id=device, device_id_type=MESH)
        copy.start()
        return copy

    def place(ref, device):
        q = count[0]
        count[0] += 1
        copy = remote(ref, ref, gs.at[q], gr.at[q], device)
        pending.append(copy)
        return copy

    for j in range(4):
        lanes = slice(LANES * j, LANES * (j + 1))
        swap[j] = points_ref[pl.ds(pl.multiple_of(other * ROWS, ROWS), ROWS), lanes]
        pts[core * 4 + j, z, x, y] = points_ref[pl.ds(pl.multiple_of(core * ROWS, ROWS), ROWS), lanes]
    count[0] += 1
    swapped = remote(swap, pts.at[pl.ds(core * 4, 4), z, x, y], gs.at[0], gr.at[0], sibling)
    pending.append(swapped)
    cbf[core] = cent_ref[...].astype(jnp.bfloat16)
    cents_in = place(cbf.at[core], sibling)
    swapped.wait_recv()

    PZ, PX, PY = pl.ds(0, 2), pl.ds(2, 3), pl.ds(5, 3)
    first = []
    for d in (4, 3, 5, 2, 6, 1, 7):
        first.append(place(pts.at[PY, z, x, y], on_z(z + d)))
    for d in (2, 1, 3):
        first.append(place(pts.at[PX, z, x, y], on_y(y + d)))
        first.append(place(pts.at[PZ, z, x, y], on_x(x + d)))
    for copy in first:
        copy.wait_recv()

    def ring(n, pos, at, sub):
        right, left = at(pos + 1), at(pos + n - 1)
        prev_r, prev_l = {}, {}
        for s in range(1, n // 2 + 1):
            last = s == n // 2
            now_r, now_l = {}, {}
            for hr, hl in ((0, 1),) if last else ((0, 1), (1, 0)):
                if s > 1:
                    prev_r[hr].wait_recv()
                now_r[hr] = place(sub(lax.rem(pos + n - s + 1, n), hr), right)
                if s > 1:
                    prev_l[hl].wait_recv()
                now_l[hl] = place(sub(lax.rem(pos + s - 1, n), hl), left)
                yield
            if last:
                prev_r[1].wait_recv()
                prev_l[0].wait_recv()
            prev_r, prev_l = now_r, now_l
        prev_r[0].wait_recv()
        prev_l[1].wait_recv()
        yield

    def run(order, rings):
        for name in order:
            next(rings[name])

    run("zzxxyyzzxyzzzxyz", {
        "z": ring(NZ, z, on_z, lambda i, h: pts.at[PX, i, x, pl.ds(2 * h, 2)]),
        "x": ring(NX, x, on_x, lambda i, h: pts.at[PY, pl.ds(4 * h, 4), i, y]),
        "y": ring(NY, y, on_y, lambda i, h: pts.at[pl.ds(h, 1), z, :, i]),
    })
    run("xxyyzzzzxyzzzzxy", {
        "z": ring(NZ, z, on_z, lambda i, h: pts.at[pl.ds(h, 1), i]),
        "x": ring(NX, x, on_x, lambda i, h: pts.at[PX, pl.ds(4 * h, 4), i]),
        "y": ring(NY, y, on_y, lambda i, h: pts.at[PY, pl.ds(4 * h, 4), :, i]),
    })
    cents_in.wait_recv()

    def logit_block(b, carry):
        acc = None
        for h in range(2):
            block = jnp.concatenate(
                [pts[4 * h + j, b].reshape(NX * NY * ROWS, LANES) for j in range(4)], axis=1)
            part = lax.dot_general(cbf[h], block, (((1,), (1,)), ((), ())), preferred_element_type=jnp.float32)
            acc = part if acc is None else acc + part
        logits[:, pl.ds(pl.multiple_of(b * 256, 256), 256)] = acc * (SCALE * math.log2(math.e))
        return carry

    lax.fori_loop(0, NZ, logit_block, 0)

    lane = lax.broadcasted_iota(jnp.int32, (8, LANES), 1)

    def compact(b, acc, column):
        for q in range(16):
            acc = jnp.where(lane == 16 * b + q, jnp.broadcast_to(column[8 * q:8 * q + 8], (8, LANES)), acc)
        return acc

    def spread(dst, value):
        for g in range(CGROUPS):
            dst[8 * g:8 * g + 8, :] = jnp.broadcast_to(value[:, g:g + 1], (8, LANES))

    def merge(parts):
        top = reduce(jnp.maximum, parts)
        return top + jnp.log2(sum(jnp.exp2(p - top) for p in parts))

    rpot[...] = jnp.zeros((PBLOCKS, LANES), jnp.float32)

    def sweep(it, carry):
        def col_block(g, c):
            rows = pl.ds(pl.multiple_of(g * 16, 16), 16)
            vals = [logits[rows, LANES * j:LANES * (j + 1)] + rpot[j:j + 1, :] for j in range(PBLOCKS)]
            top = reduce(jnp.maximum, vals)
            col_max[rows, :] = top
            col_sum[rows, :] = sum(jnp.exp2(v - top) for v in vals)
            return c

        lax.fori_loop(0, CENTS // 16, col_block, 0)

        def col_finish(b, acc):
            rows = pl.ds(pl.multiple_of(b * 128, 128), 128)
            lane_max = col_max[rows, :]
            top = jnp.max(lane_max, axis=1, keepdims=True)
            total = jnp.sum(col_sum[rows, :] * jnp.exp2(lane_max - top), axis=1, keepdims=True)
            return compact(b, acc, top + jnp.log2(total))

        mine = lax.fori_loop(0, CENTS // 128, col_finish, jnp.zeros((8, LANES), jnp.float32))
        csend[it] = mine
        pair = remote(csend.at[it], crecv.at[it], its.at[it, STAGE_SEMS - 1], itr.at[it, STAGE_SEMS - 1], sibling)
        pair.wait_recv()
        spread(cpot, -LOG2_CENTS - merge([mine, crecv[it]]))

        for jb in range(4):
            def row_block(q, carry):
                tops, sums = carry
                rows = pl.ds(pl.multiple_of(q * 64, 64), 64)
                pot = cpot[rows, :].reshape(8, 8, LANES)
                new_tops, new_sums = [], []
                for j in range(4):
                    lanes = slice(512 * jb + LANES * j, 512 * jb + LANES * (j + 1))
                    vals = logits[rows, lanes].reshape(8, 8, LANES) + pot
                    top = jnp.maximum(tops[j], jnp.max(vals, axis=0))
                    new_sums.append(sums[j] * jnp.exp2(tops[j] - top) + jnp.sum(jnp.exp2(vals - top[None]), axis=0))
                    new_tops.append(top)
                return tuple(new_tops), tuple(new_sums)

            low = tuple(jnp.full((8, LANES), -3e38, jnp.float32) for _ in range(4))
            none = tuple(jnp.zeros((8, LANES), jnp.float32) for _ in range(4))
            tops, sums = lax.fori_loop(0, CENTS // 64, row_block, (low, none))
            for j in range(4):
                top = jnp.max(tops[j], axis=0, keepdims=True)
                total = jnp.sum(sums[j] * jnp.exp2(tops[j] - top), axis=0, keepdims=True)
                rsend[it, 0, 4 * jb + j:4 * jb + j + 1, :] = top + jnp.log2(total)

        merged = None
        sent = [pair]
        for k, (base, n) in enumerate(STAGES):
            pos, at = ((y, on_y), (x, on_x), (z, on_z))[k]
            if k:
                rsend[it, k] = merged
            copies = []
            for d in sorted(range(1, n), key=lambda d: -min(d, n - d)):
                q = base + d - 1
                copies.append(remote(rsend.at[it, k], rrecv.at[it, q], its.at[it, q], itr.at[it, q], at(pos + d)))
            for copy in copies:
                copy.wait_recv()
            merged = merge([rsend[it, k]] + [rrecv[it, base + d] for d in range(n - 1)])
            sent += copies
        rpot[...] = -LOG2_POINTS - merged
        for copy in sent:
            copy.wait_send()
        return carry

    lax.fori_loop(0, ITERS, sweep, 0)

    def plan_block(g, c):
        rows = pl.ds(pl.multiple_of(g * 16, 16), 16)
        pot = cpot[rows, :] + LOG2_POINTS
        total = None
        for j in range(PBLOCKS):
            lanes = slice(LANES * j, LANES * (j + 1))
            value = jnp.exp2(logits[rows, lanes] + rpot[j:j + 1, :] + pot)
            weights[rows, lanes] = value.astype(jnp.bfloat16)
            total = value if total is None else total + value
        col_sum[rows, :] = total
        return c

    lax.fori_loop(0, CENTS // 16, plan_block, 0)

    def mass_finish(b, acc):
        rows = pl.ds(pl.multiple_of(b * 128, 128), 128)
        return compact(b, acc, jnp.sum(col_sum[rows, :], axis=1, keepdims=True))

    mine = lax.fori_loop(0, CENTS // 128, mass_finish, jnp.zeros((8, LANES), jnp.float32))
    msend[...] = mine
    mass_in = remote(msend, mrecv, fs.at[2], fr.at[2], sibling)

    def product(tile):
        block = jnp.concatenate([pts[tile + j].reshape(PTS, LANES) for j in range(2)], axis=1)
        return jnp.dot(weights[...], block, preferred_element_type=jnp.float32)

    partial_in = []
    for b in range(2):
        nsend[b] = product(other * 4 + 2 * b)
        partial_in.append(remote(nsend.at[b], nrecv.at[b], fs.at[b], fr.at[b], sibling))

    mass_in.wait_recv()
    spread(col_sum, mine + mrecv[...])
    diagonal = (lax.broadcasted_iota(jnp.int32, (LANES, LANES), 0)
                == lax.broadcasted_iota(jnp.int32, (LANES, LANES), 1))
    for b in range(8):
        mass_ref[b:b + 1, :] = jnp.sum(
            jnp.where(diagonal, col_sum[LANES * b:LANES * (b + 1), :], 0.0), axis=0, keepdims=True)

    for b in range(2):
        lanes = slice(256 * b, 256 * (b + 1))
        own = product(core * 4 + 2 * b)
        partial_in[b].wait_recv()
        scale = 1.0 / (col_sum[...] + PRIOR)
        out_ref[:, lanes] = (own + nrecv[b] + PRIOR * cent_ref[:, lanes]) * jnp.concatenate([scale, scale], axis=1)

    for copy in pending + partial_in + [mass_in]:
        copy.wait_send()


def per_device(points, centroids):
    vmem = pl.BlockSpec(memory_space=pltpu.VMEM)
    f32, bf16 = jnp.float32, jnp.bfloat16
    fresh, mass = pl.pallas_call(
        kernel,
        out_shape=(jax.ShapeDtypeStruct((CENTS, HALF), f32), jax.ShapeDtypeStruct((8, LANES), f32)),
        in_specs=[vmem, vmem],
        out_specs=(vmem, vmem),
        scratch_shapes=[
            pltpu.VMEM((TILES, NZ, NX, NY, ROWS, LANES), bf16),
            pltpu.VMEM((4, ROWS, LANES), bf16),
            pltpu.VMEM((2, CENTS, HALF), bf16),
            pltpu.VMEM((CENTS, PTS), f32),
            pltpu.VMEM((CENTS, PTS), bf16),
            pltpu.VMEM((CENTS, LANES), f32),
            pltpu.VMEM((CENTS, LANES), f32),
            pltpu.VMEM((CENTS, LANES), f32),
            pltpu.VMEM((PBLOCKS, LANES), f32),
            pltpu.VMEM((ITERS, 8, LANES), f32),
            pltpu.VMEM((ITERS, 8, LANES), f32),
            pltpu.VMEM((ITERS, 3, PBLOCKS, LANES), f32),
            pltpu.VMEM((ITERS, STAGE_SEMS - 1, PBLOCKS, LANES), f32),
            pltpu.VMEM((8, LANES), f32),
            pltpu.VMEM((8, LANES), f32),
            pltpu.VMEM((2, CENTS, 256), f32),
            pltpu.VMEM((2, CENTS, 256), f32),
            pltpu.SemaphoreType.DMA((GATHER_SEMS,)),
            pltpu.SemaphoreType.DMA((GATHER_SEMS,)),
            pltpu.SemaphoreType.DMA((ITERS, STAGE_SEMS)),
            pltpu.SemaphoreType.DMA((ITERS, STAGE_SEMS)),
            pltpu.SemaphoreType.DMA((3,)),
            pltpu.SemaphoreType.DMA((3,)),
        ],
        compiler_params=pltpu.CompilerParams(
            collective_id=0, has_side_effects=True, vmem_limit_bytes=60 * 1024 * 1024),
    )(points, centroids)
    return fresh, mass.reshape(CENTS)


def solution(mesh):
    return jax.shard_map(
        per_device,
        mesh=mesh,
        in_specs=(P("blk", "rep"), P("blk", "rep")),
        out_specs=(P("blk", "rep"), P("blk")),
        check_vma=False,
    )
```

```python
import math
from functools import reduce

import jax
import jax.numpy as jnp
from jax import lax
from jax.experimental import pallas as pl
from jax.experimental.pallas import tpu as pltpu
from jax.sharding import PartitionSpec as P

ITERS = 3
SCALE = 3.0
NZ, NX, NY = 8, 4, 4
CENTS = 1024
HALF = 512
ROWS = 16
PTS = NZ * NX * NY * ROWS
TILES = 8
LANES = 128
PBLOCKS = PTS // LANES
CGROUPS = CENTS // 8
LOG2_POINTS = 12.0
LOG2_CENTS = 17.0
PRIOR = 4096 / 131072
MESH = pl.DeviceIdType.MESH
GATHER_SEMS = 134
PLANE = tuple((dx, dy) for dx in range(NX) for dy in range(NY) if dx or dy)
STAGES = ((0, len(PLANE)), (len(PLANE), NZ - 1))
STAGE_SEMS = len(PLANE) + NZ


def kernel(points_hbm, cent_hbm, out_ref, mass_ref, points_ref, cent_ref, pts, swap, cbf, logits, weights,
           col_max, col_sum, cpot, rpot, csend, crecv, rsend, rrecv, msend, mrecv, nsend, nrecv,
           gs, gr, its, itr, fs, fr, ls):
    blk = lax.axis_index("blk")
    core = lax.axis_index("rep")
    other = 1 - core
    z = lax.div(blk, NX * NY)
    x = lax.rem(lax.div(blk, NY), NX)
    y = lax.rem(blk, NY)

    def at(dz, dx, dy):
        return (lax.rem(z + dz, NZ) * (NX * NY) + lax.rem(x + dx, NX) * NY + lax.rem(y + dy, NY), core)

    sibling = (blk, other)

    points_in = pltpu.make_async_copy(points_hbm, points_ref, ls.at[0])
    points_in.start()
    own_in = pltpu.make_async_copy(cent_hbm, cent_ref, ls.at[1])
    own_in.start()
    barrier = pltpu.get_barrier_semaphore()
    pl.semaphore_signal(barrier, inc=1, device_id=sibling, device_id_type=MESH)
    for dx, dy in PLANE:
        pl.semaphore_signal(barrier, inc=1, device_id=at(0, dx, dy), device_id_type=MESH)
    for d in range(1, NZ):
        pl.semaphore_signal(barrier, inc=1, device_id=at(d, 0, 0), device_id_type=MESH)
    points_in.wait()
    for j in range(4):
        lanes = slice(LANES * j, LANES * (j + 1))
        swap[j] = points_ref[pl.ds(pl.multiple_of(other * ROWS, ROWS), ROWS), lanes]
        pts[core * 4 + j, z, x, y] = points_ref[pl.ds(pl.multiple_of(core * ROWS, ROWS), ROWS), lanes]
    pl.semaphore_wait(barrier, STAGE_SEMS)

    pending = []
    count = [0]

    def remote(src, dst, send_sem, recv_sem, device):
        copy = pltpu.make_async_remote_copy(
            src_ref=src, dst_ref=dst, send_sem=send_sem, recv_sem=recv_sem,
            device_id=device, device_id_type=MESH)
        copy.start()
        return copy

    def place(ref, device):
        q = count[0]
        count[0] += 1
        copy = remote(ref, ref, gs.at[q], gr.at[q], device)
        pending.append(copy)
        return copy

    count[0] += 1
    swapped = remote(swap, pts.at[pl.ds(core * 4, 4), z, x, y], gs.at[0], gr.at[0], sibling)
    pending.append(swapped)
    own_in.wait()
    cbf[core] = cent_ref[...].astype(jnp.bfloat16)
    cents_in = place(cbf.at[core], sibling)
    swapped.wait_recv()

    PZ, PX, PY, PXY = pl.ds(0, 2), pl.ds(2, 3), pl.ds(5, 3), pl.ds(2, 6)
    along_z = {}
    for d in (4, 3, 5, 2, 6, 1, 7):
        along_z[NZ - d] = place(pts.at[PXY, z, x, y], at(d, 0, 0))
    second, third, fourth, tasks = {}, {}, {}, []

    def spread_layer(dz):
        if dz:
            along_z[dz].wait_recv()
        layer = lax.rem(z + dz, NZ)
        second[dz] = []
        for d in (2, 1, 3):
            second[dz].append(place(pts.at[PX, layer, x, y], at(0, 0, d)))
            second[dz].append(place(pts.at[PY, layer, x, y], at(0, d, 0)))

    def x_line(dz, dx):
        return pts.at[PX, lax.rem(z + dz, NZ), lax.rem(x + dx, NX)]

    def y_line(dz, dy):
        return pts.at[PY, lax.rem(z + dz, NZ), :, lax.rem(y + dy, NY)]

    def send_lines(dz):
        for copy in second[dz]:
            copy.wait_recv()
        third[dz] = {}
        for d in (1, 3):
            third[dz]["x", d] = place(x_line(dz, 0), at(0, d, 0))
            third[dz]["y", d] = place(y_line(dz, 0), at(0, 0, d))

    def forward_lines(dz):
        d = 1 if dz % 2 else 3
        third[dz]["x", d].wait_recv()
        right = place(x_line(dz, NX - d), at(0, d, 0))
        third[dz]["y", d].wait_recv()
        fourth[dz] = (right, place(y_line(dz, NY - d), at(0, 0, d)))

    def layer_done(dz):
        d = 3 if dz % 2 else 1
        third[dz]["x", d].wait_recv()
        third[dz]["y", d].wait_recv()
        for copy in fourth[dz]:
            copy.wait_recv()

    def z_ring():
        def block(d, h):
            return pts.at[pl.ds(h, 1), lax.rem(z + d, NZ)]

        up, down = at(1, 0, 0), at(NZ - 1, 0, 0)
        prev_u, prev_d = {}, {}
        for s in range(1, NZ // 2 + 1):
            last = s == NZ // 2
            now_u, now_d = {}, {}
            for hu, hd in ((0, 1),) if last else ((0, 1), (1, 0)):
                if s > 1:
                    prev_u[hu].wait_recv()
                now_u[hu] = place(block(NZ - s + 1, hu), up)
                if s > 1:
                    prev_d[hd].wait_recv()
                now_d[hd] = place(block(s - 1, hd), down)
            if last:
                prev_u[1].wait_recv()
                prev_d[0].wait_recv()
            prev_u, prev_d = now_u, now_d
            yield
        prev_u[0].wait_recv()
        prev_d[1].wait_recv()
        yield

    ring = z_ring()
    spread_layer(0)
    plane = [place(pts.at[PZ, z, x, y], at(0, dx, dy)) for dx, dy in PLANE]

    def plane_done():
        for copy in plane:
            copy.wait_recv()
        next(ring)

    def logit_block(dz):
        layer = lax.rem(z + dz, NZ)
        acc = None
        for h in range(2):
            block = jnp.concatenate(
                [pts[4 * h + j, layer].reshape(NX * NY * ROWS, LANES) for j in range(4)], axis=1)
            part = lax.dot_general(cbf[h], block, (((1,), (1,)), ((), ())), preferred_element_type=jnp.float32)
            acc = part if acc is None else acc + part
        logits[:, pl.ds(pl.multiple_of(layer * 256, 256), 256)] = acc * (SCALE * math.log2(math.e))

    near, far = {0: 0, 1: 1, 7: 1, 2: 2, 6: 2, 3: 3, 5: 3, 4: 4}, (0, 1, 7, 2, 6, 3, 5, 4)
    for dz in far:
        r = near[dz]
        if dz:
            tasks.append(((0, 3.5, 4.3, 5.2, 6.0)[r], spread_layer, (dz,)))
        tasks.append(((3.9, 7.3, 8.2, 9.2, 10.2)[r], send_lines, (dz,)))
        tasks.append(((7.4, 10.9, 11.8, 13.0, 14.0)[r], forward_lines, (dz,)))
        tasks.append(((10.95, 14.8, 15.5, 16.5, 18.2)[r], layer_done, (dz,)))
        tasks.append(((10.95, 14.8, 15.5, 16.5, 18.2)[r], logit_block, (dz,)))
    tasks.append((5.1, plane_done, ()))
    for t in (8.3, 11.5, 14.6, 18.1):
        tasks.append((t, next, (ring,)))
    tasks.append((10.9, cents_in.wait_recv, ()))
    for _, task, args in sorted(tasks, key=lambda t: t[0]):
        task(*args)

    lane = lax.broadcasted_iota(jnp.int32, (8, LANES), 1)

    def compact(column):
        acc = jnp.zeros((8, LANES), jnp.float32)
        for g in range(CGROUPS):
            acc = jnp.where(lane == g, jnp.broadcast_to(column[8 * g:8 * g + 8], (8, LANES)), acc)
        return acc

    def spread(dst, value):
        for g in range(CGROUPS):
            dst[8 * g:8 * g + 8, :] = jnp.broadcast_to(value[:, g:g + 1], (8, LANES))

    def merge(parts):
        top = reduce(jnp.maximum, parts)
        return top + jnp.log2(sum(jnp.exp2(p - top) for p in parts))

    rpot[...] = jnp.zeros((PBLOCKS, LANES), jnp.float32)

    def sweep(it, carry):
        def col_block(g, c):
            rows = pl.ds(pl.multiple_of(g * 16, 16), 16)
            vals = [logits[rows, LANES * j:LANES * (j + 1)] + rpot[j:j + 1, :] for j in range(PBLOCKS)]
            top = reduce(jnp.maximum, vals)
            col_max[rows, :] = top
            col_sum[rows, :] = sum(jnp.exp2(v - top) for v in vals)
            return c

        lax.fori_loop(0, CENTS // 16, col_block, 0, unroll=4)

        top = jnp.max(col_max[...], axis=1, keepdims=True)
        total = jnp.sum(col_sum[...] * jnp.exp2(col_max[...] - top), axis=1, keepdims=True)
        mine = compact(top + jnp.log2(total))
        csend[it] = mine
        pair = remote(csend.at[it], crecv.at[it], its.at[it, STAGE_SEMS - 1], itr.at[it, STAGE_SEMS - 1], sibling)
        pair.wait_recv()
        spread(cpot, -LOG2_CENTS - merge([mine, crecv[it]]))

        for jb in range(4):
            def row_block(q, carry):
                tops, sums = carry
                rows = pl.ds(pl.multiple_of(q * 64, 64), 64)
                pot = cpot[rows, :].reshape(8, 8, LANES)
                new_tops, new_sums = [], []
                for j in range(4):
                    lanes = slice(512 * jb + LANES * j, 512 * jb + LANES * (j + 1))
                    vals = logits[rows, lanes].reshape(8, 8, LANES) + pot
                    top = jnp.maximum(tops[j], jnp.max(vals, axis=0))
                    new_sums.append(sums[j] * jnp.exp2(tops[j] - top) + jnp.sum(jnp.exp2(vals - top[None]), axis=0))
                    new_tops.append(top)
                return tuple(new_tops), tuple(new_sums)

            low = tuple(jnp.full((8, LANES), -3e38, jnp.float32) for _ in range(4))
            none = tuple(jnp.zeros((8, LANES), jnp.float32) for _ in range(4))
            tops, sums = lax.fori_loop(0, CENTS // 64, row_block, (low, none), unroll=4)
            for j in range(4):
                top = jnp.max(tops[j], axis=0, keepdims=True)
                total = jnp.sum(sums[j] * jnp.exp2(tops[j] - top), axis=0, keepdims=True)
                rsend[it, 0, 4 * jb + j:4 * jb + j + 1, :] = top + jnp.log2(total)

        merged = None
        sent = [pair]
        for k, (base, n) in enumerate(STAGES):
            peers = [at(0, dx, dy) for dx, dy in PLANE] if k == 0 else [at(d, 0, 0) for d in range(1, NZ)]
            if k:
                rsend[it, k] = merged
            copies = [remote(rsend.at[it, k], rrecv.at[it, base + q], its.at[it, base + q], itr.at[it, base + q], peer)
                      for q, peer in enumerate(peers)]
            for copy in copies:
                copy.wait_recv()
            merged = merge([rsend[it, k]] + [rrecv[it, base + q] for q in range(n)])
            sent += copies
        rpot[...] = -LOG2_POINTS - merged
        for copy in sent:
            copy.wait_send()
        return carry

    lax.fori_loop(0, ITERS, sweep, 0)

    def plan_block(g, c):
        rows = pl.ds(pl.multiple_of(g * 16, 16), 16)
        pot = cpot[rows, :] + LOG2_POINTS
        total = None
        for j in range(PBLOCKS):
            lanes = slice(LANES * j, LANES * (j + 1))
            value = jnp.exp2(logits[rows, lanes] + rpot[j:j + 1, :] + pot)
            weights[rows, lanes] = value.astype(jnp.bfloat16)
            total = value if total is None else total + value
        col_sum[rows, :] = total
        return c

    lax.fori_loop(0, CENTS // 16, plan_block, 0, unroll=4)

    mine = compact(jnp.sum(col_sum[...], axis=1, keepdims=True))
    msend[...] = mine
    mass_in = remote(msend, mrecv, fs.at[2], fr.at[2], sibling)

    def product(tile):
        block = jnp.concatenate([pts[tile + j].reshape(PTS, LANES) for j in range(2)], axis=1)
        return jnp.dot(weights[...], block, preferred_element_type=jnp.float32)

    partial_in = []
    for b in range(2):
        nsend[b] = product(other * 4 + 2 * b)
        partial_in.append(remote(nsend.at[b], nrecv.at[b], fs.at[b], fr.at[b], sibling))

    mass_in.wait_recv()
    spread(col_sum, mine + mrecv[...])
    diagonal = (lax.broadcasted_iota(jnp.int32, (LANES, LANES), 0)
                == lax.broadcasted_iota(jnp.int32, (LANES, LANES), 1))
    for b in range(8):
        mass_ref[b:b + 1, :] = jnp.sum(
            jnp.where(diagonal, col_sum[LANES * b:LANES * (b + 1), :], 0.0), axis=0, keepdims=True)

    for b in range(2):
        lanes = slice(256 * b, 256 * (b + 1))
        own = product(core * 4 + 2 * b)
        partial_in[b].wait_recv()
        scale = 1.0 / (col_sum[...] + PRIOR)
        out_ref[:, lanes] = (own + nrecv[b] + PRIOR * cent_ref[:, lanes]) * jnp.concatenate([scale, scale], axis=1)

    for copy in pending + partial_in + [mass_in]:
        copy.wait_send()


def per_device(points, centroids):
    vmem = pl.BlockSpec(memory_space=pltpu.VMEM)
    hbm = pl.BlockSpec(memory_space=pl.ANY)
    f32, bf16 = jnp.float32, jnp.bfloat16
    fresh, mass = pl.pallas_call(
        kernel,
        out_shape=(jax.ShapeDtypeStruct((CENTS, HALF), f32), jax.ShapeDtypeStruct((8, LANES), f32)),
        in_specs=[hbm, hbm],
        out_specs=(vmem, vmem),
        scratch_shapes=[
            pltpu.VMEM((2 * ROWS, HALF), bf16),
            pltpu.VMEM((CENTS, HALF), f32),
            pltpu.VMEM((TILES, NZ, NX, NY, ROWS, LANES), bf16),
            pltpu.VMEM((4, ROWS, LANES), bf16),
            pltpu.VMEM((2, CENTS, HALF), bf16),
            pltpu.VMEM((CENTS, PTS), f32),
            pltpu.VMEM((CENTS, PTS), bf16),
            pltpu.VMEM((CENTS, LANES), f32),
            pltpu.VMEM((CENTS, LANES), f32),
            pltpu.VMEM((CENTS, LANES), f32),
            pltpu.VMEM((PBLOCKS, LANES), f32),
            pltpu.VMEM((ITERS, 8, LANES), f32),
            pltpu.VMEM((ITERS, 8, LANES), f32),
            pltpu.VMEM((ITERS, len(STAGES), PBLOCKS, LANES), f32),
            pltpu.VMEM((ITERS, STAGE_SEMS - 1, PBLOCKS, LANES), f32),
            pltpu.VMEM((8, LANES), f32),
            pltpu.VMEM((8, LANES), f32),
            pltpu.VMEM((2, CENTS, 256), f32),
            pltpu.VMEM((2, CENTS, 256), f32),
            pltpu.SemaphoreType.DMA((GATHER_SEMS,)),
            pltpu.SemaphoreType.DMA((GATHER_SEMS,)),
            pltpu.SemaphoreType.DMA((ITERS, STAGE_SEMS)),
            pltpu.SemaphoreType.DMA((ITERS, STAGE_SEMS)),
            pltpu.SemaphoreType.DMA((3,)),
            pltpu.SemaphoreType.DMA((3,)),
            pltpu.SemaphoreType.DMA((2,)),
        ],
        compiler_params=pltpu.CompilerParams(
            collective_id=0, has_side_effects=True, vmem_limit_bytes=60 * 1024 * 1024),
    )(points, centroids)
    return fresh, mass.reshape(CENTS)


def solution(mesh):
    return jax.shard_map(
        per_device,
        mesh=mesh,
        in_specs=(P("blk", "rep"), P("blk", "rep")),
        out_specs=(P("blk", "rep"), P("blk")),
        check_vma=False,
    )
```

```python
import math
from functools import reduce

import jax
import jax.numpy as jnp
from jax import lax
from jax.experimental import pallas as pl
from jax.experimental.pallas import tpu as pltpu
from jax.sharding import PartitionSpec as P

ITERS = 3
SCALE = 3.0
NZ, NX, NY = 8, 4, 4
CENTS = 1024
HALF = 512
ROWS = 16
PTS = NZ * NX * NY * ROWS
TILES = 8
LANES = 128
PBLOCKS = PTS // LANES
CGROUPS = CENTS // 8
LOG2_POINTS = 12.0
LOG2_CENTS = 17.0
PRIOR = 4096 / 131072
CHUNK = 256
MESH = pl.DeviceIdType.MESH
GATHER_SEMS = 148
PLANE = tuple((dx, dy) for dx in range(NX) for dy in range(NY) if dx or dy)
STAGES = ((0, len(PLANE)), (len(PLANE), NZ - 1))
STAGE_SEMS = len(PLANE) + NZ


def kernel(points_hbm, cent_hbm, out_ref, mass_ref, points_ref, cent_ref, pts, swap, cbf, logits, weights,
           col_max, col_sum, cpot, rpot, csend, crecv, rsend, rrecv, msend, mrecv, nsend, nrecv, own, fresh,
           gs, gr, its, itr, fs, fr, ls):
    blk = lax.axis_index("blk")
    core = lax.axis_index("rep")
    other = 1 - core
    z = lax.div(blk, NX * NY)
    x = lax.rem(lax.div(blk, NY), NX)
    y = lax.rem(blk, NY)

    def at(dz, dx, dy):
        return (lax.rem(z + dz, NZ) * (NX * NY) + lax.rem(x + dx, NX) * NY + lax.rem(y + dy, NY), core)

    sibling = (blk, other)

    points_in = pltpu.make_async_copy(points_hbm, points_ref, ls.at[0])
    points_in.start()
    own_in = pltpu.make_async_copy(cent_hbm, cent_ref, ls.at[1])
    own_in.start()
    barrier = pltpu.get_barrier_semaphore()
    pl.semaphore_signal(barrier, inc=1, device_id=sibling, device_id_type=MESH)
    for dx, dy in PLANE:
        pl.semaphore_signal(barrier, inc=1, device_id=at(0, dx, dy), device_id_type=MESH)
    for d in range(1, NZ):
        pl.semaphore_signal(barrier, inc=1, device_id=at(d, 0, 0), device_id_type=MESH)
    points_in.wait()
    for j in range(4):
        lanes = slice(LANES * j, LANES * (j + 1))
        swap[j] = points_ref[pl.ds(pl.multiple_of(other * ROWS, ROWS), ROWS), lanes]
        pts[core * 4 + j, z, x, y] = points_ref[pl.ds(pl.multiple_of(core * ROWS, ROWS), ROWS), lanes]
    pl.semaphore_wait(barrier, STAGE_SEMS)

    pending = []
    count = [0]

    def remote(src, dst, send_sem, recv_sem, device):
        copy = pltpu.make_async_remote_copy(
            src_ref=src, dst_ref=dst, send_sem=send_sem, recv_sem=recv_sem,
            device_id=device, device_id_type=MESH)
        copy.start()
        return copy

    def place(ref, device):
        q = count[0]
        count[0] += 1
        copy = remote(ref, ref, gs.at[q], gr.at[q], device)
        pending.append(copy)
        return copy

    count[0] += 1
    swapped = remote(swap, pts.at[pl.ds(core * 4, 4), z, x, y], gs.at[0], gr.at[0], sibling)
    pending.append(swapped)
    own_in.wait()
    cbf[core] = cent_ref[...].astype(jnp.bfloat16)
    cents_in = place(cbf.at[core], sibling)
    swapped.wait_recv()

    PZ, PX, PY, PXY = pl.ds(0, 2), pl.ds(2, 3), pl.ds(5, 3), pl.ds(2, 6)
    along_z = {}
    second, third, fourth = {}, {}, {}

    def spread_layer(dz):
        if dz:
            along_z[dz].wait_recv()
        layer = lax.rem(z + dz, NZ)
        second[dz] = []
        for d in (2, 1, 3):
            second[dz].append(place(pts.at[PX, layer, x, y], at(0, 0, d)))
            second[dz].append(place(pts.at[PY, layer, x, y], at(0, d, 0)))

    def x_line(dz, dx):
        return pts.at[PX, lax.rem(z + dz, NZ), lax.rem(x + dx, NX)]

    def y_line(dz, dy):
        return pts.at[PY, lax.rem(z + dz, NZ), :, lax.rem(y + dy, NY)]

    def send_lines(dz):
        for copy in second[dz]:
            copy.wait_recv()
        third[dz] = {}
        for d in (1, 3):
            third[dz]["x", d] = place(x_line(dz, 0), at(0, d, 0))
            third[dz]["y", d] = place(y_line(dz, 0), at(0, 0, d))

    def forward_lines(dz):
        d = 1 if dz % 2 else 3
        third[dz]["x", d].wait_recv()
        right = place(x_line(dz, NX - d), at(0, d, 0))
        third[dz]["y", d].wait_recv()
        fourth[dz] = (right, place(y_line(dz, NY - d), at(0, 0, d)))

    def layer_done(dz):
        d = 3 if dz % 2 else 1
        third[dz]["x", d].wait_recv()
        third[dz]["y", d].wait_recv()
        for copy in fourth[dz]:
            copy.wait_recv()

    def z_block(d, c):
        return pts.at[PZ, lax.rem(z + d, NZ), lax.rem(x + c, NX)]

    plane, up, down = {}, {}, {}

    def z_step(s, c):
        if s > 1:
            up[s - 1, c].wait_recv()
            down[s - 1, c].wait_recv()
        else:
            for copy in plane[c]:
                copy.wait_recv()
        if s < NZ // 2 or c < 2:
            up[s, c] = place(z_block(NZ - s + 1, c), at(1, 0, 0))
        if s < NZ // 2 or c >= 2:
            down[s, c] = place(z_block(s - 1, c), at(NZ - 1, 0, 0))

    for d in (1, 7, 2, 6, 3, 5, 4):
        along_z[NZ - d] = place(pts.at[PXY, z, x, y], at(d, 0, 0))
    spread_layer(0)
    for dx in (0, 2, 1, 3):
        plane[(NX - dx) % NX] = [place(pts.at[PZ, z, x, y], at(0, dx, dy)) for dy in range(NY) if dx or dy]

    def logit_block(dz):
        layer_done(dz)
        if dz == 0:
            cents_in.wait_recv()
        elif dz == NZ // 2:
            for copy in (up[dz, 0], up[dz, 1], down[dz, 2], down[dz, 3]):
                copy.wait_recv()
        layer = lax.rem(z + dz, NZ)
        lanes = pl.ds(pl.multiple_of(layer * 256, 256), 256)

        def part(m, carry):
            rows = pl.ds(pl.multiple_of(m * CHUNK, CHUNK), CHUNK)
            acc = None
            for h in range(2):
                block = jnp.concatenate(
                    [pts[4 * h + j, layer].reshape(NX * NY * ROWS, LANES) for j in range(4)], axis=1)
                term = lax.dot_general(
                    cbf[h, rows, :], block, (((1,), (1,)), ((), ())), preferred_element_type=jnp.float32)
                acc = term if acc is None else acc + term
            logits[rows, lanes] = acc * (SCALE * math.log2(math.e))
            return carry

        lax.fori_loop(0, CENTS // CHUNK, part, 0)

    tasks = {"a": spread_layer, "b": send_lines, "c": forward_lines, "r": z_step, "m": logit_block}
    for step in (
        ("a", 1), ("a", 7), ("b", 0), ("r", 1, 0), ("r", 1, 1), ("r", 1, 3), ("r", 1, 2), ("a", 2), ("a", 6), ("b", 1),
        ("b", 7), ("a", 3), ("a", 5), ("c", 0), ("r", 2, 0), ("r", 2, 1), ("r", 2, 3), ("r", 2, 2), ("a", 4), ("b", 2),
        ("b", 6), ("c", 1), ("c", 7), ("m", 0), ("b", 3), ("b", 5), ("r", 3, 0), ("r", 3, 1), ("r", 3, 3), ("r", 3, 2),
        ("c", 2), ("c", 6), ("m", 1), ("m", 7), ("b", 4), ("r", 4, 0), ("r", 4, 1), ("r", 4, 3), ("r", 4, 2), ("c", 3),
        ("c", 5), ("m", 2), ("m", 6), ("c", 4), ("m", 3), ("m", 5), ("m", 4),
    ):
        tasks[step[0]](*step[1:])

    lane = lax.broadcasted_iota(jnp.int32, (8, LANES), 1)

    def compact(column):
        acc = jnp.zeros((8, LANES), jnp.float32)
        for g in range(CGROUPS):
            acc = jnp.where(lane == g, jnp.broadcast_to(column[8 * g:8 * g + 8], (8, LANES)), acc)
        return acc

    def spread(dst, value):
        for g in range(CGROUPS):
            dst[8 * g:8 * g + 8, :] = jnp.broadcast_to(value[:, g:g + 1], (8, LANES))

    def merge(parts):
        top = reduce(jnp.maximum, parts)
        return top + jnp.log2(sum(jnp.exp2(p - top) for p in parts))

    rpot[...] = jnp.zeros((PBLOCKS, LANES), jnp.float32)

    def sweep(it, carry):
        def col_block(g, c):
            rows = pl.ds(pl.multiple_of(g * 16, 16), 16)
            vals = [logits[rows, LANES * j:LANES * (j + 1)] + rpot[j:j + 1, :] for j in range(PBLOCKS)]
            top = reduce(jnp.maximum, vals)
            col_max[rows, :] = top
            col_sum[rows, :] = sum(jnp.exp2(v - top) for v in vals)
            return c

        lax.fori_loop(0, CENTS // 16, col_block, 0, unroll=4)

        top = jnp.max(col_max[...], axis=1, keepdims=True)
        total = jnp.sum(col_sum[...] * jnp.exp2(col_max[...] - top), axis=1, keepdims=True)
        mine = compact(top + jnp.log2(total))
        csend[it] = mine
        pair = remote(csend.at[it], crecv.at[it], its.at[it, STAGE_SEMS - 1], itr.at[it, STAGE_SEMS - 1], sibling)
        pair.wait_recv()
        spread(cpot, -LOG2_CENTS - merge([mine, crecv[it]]))

        for jb in range(4):
            def row_block(q, carry):
                tops, sums = carry
                rows = pl.ds(pl.multiple_of(q * 64, 64), 64)
                pot = cpot[rows, :].reshape(8, 8, LANES)
                new_tops, new_sums = [], []
                for j in range(4):
                    lanes = slice(512 * jb + LANES * j, 512 * jb + LANES * (j + 1))
                    vals = logits[rows, lanes].reshape(8, 8, LANES) + pot
                    top = jnp.maximum(tops[j], jnp.max(vals, axis=0))
                    new_sums.append(sums[j] * jnp.exp2(tops[j] - top) + jnp.sum(jnp.exp2(vals - top[None]), axis=0))
                    new_tops.append(top)
                return tuple(new_tops), tuple(new_sums)

            low = tuple(jnp.full((8, LANES), -3e38, jnp.float32) for _ in range(4))
            none = tuple(jnp.zeros((8, LANES), jnp.float32) for _ in range(4))
            tops, sums = lax.fori_loop(0, CENTS // 64, row_block, (low, none), unroll=4)
            for j in range(4):
                top = jnp.max(tops[j], axis=0, keepdims=True)
                total = jnp.sum(sums[j] * jnp.exp2(tops[j] - top), axis=0, keepdims=True)
                rsend[it, 0, 4 * jb + j:4 * jb + j + 1, :] = top + jnp.log2(total)

        merged = None
        sent = [pair]
        for k, (base, n) in enumerate(STAGES):
            peers = [at(0, dx, dy) for dx, dy in PLANE] if k == 0 else [at(d, 0, 0) for d in range(1, NZ)]
            if k:
                rsend[it, k] = merged
            copies = [remote(rsend.at[it, k], rrecv.at[it, base + q], its.at[it, base + q], itr.at[it, base + q], peer)
                      for q, peer in enumerate(peers)]
            for copy in copies:
                copy.wait_recv()
            merged = merge([rsend[it, k]] + [rrecv[it, base + q] for q in range(n)])
            sent += copies
        rpot[...] = -LOG2_POINTS - merged
        for copy in sent:
            copy.wait_send()
        return carry

    lax.fori_loop(0, ITERS, sweep, 0)

    def plan_block(g, c):
        rows = pl.ds(pl.multiple_of(g * 16, 16), 16)
        pot = cpot[rows, :] + LOG2_POINTS
        total = None
        for j in range(PBLOCKS):
            lanes = slice(LANES * j, LANES * (j + 1))
            value = jnp.exp2(logits[rows, lanes] + rpot[j:j + 1, :] + pot)
            weights[rows, lanes] = value.astype(jnp.bfloat16)
            total = value if total is None else total + value
        col_sum[rows, :] = total
        return c

    lax.fori_loop(0, CENTS // 16, plan_block, 0, unroll=4)

    mine = compact(jnp.sum(col_sum[...], axis=1, keepdims=True))
    msend[...] = mine
    mass_in = remote(msend, mrecv, fs.at[2], fr.at[2], sibling)

    def product(tile, dst):
        block = jnp.concatenate([pts[tile + j].reshape(PTS, LANES) for j in range(2)], axis=1)

        def part(m, carry):
            rows = pl.ds(pl.multiple_of(m * CHUNK, CHUNK), CHUNK)
            dst[rows, :] = jnp.dot(weights[rows, :], block, preferred_element_type=jnp.float32)
            return carry

        lax.fori_loop(0, CENTS // CHUNK, part, 0)

    partial_in = []
    for b in range(2):
        product(other * 4 + 2 * b, nsend.at[b])
        partial_in.append(remote(nsend.at[b], nrecv.at[b], fs.at[b], fr.at[b], sibling))

    mass_in.wait_recv()
    spread(col_sum, mine + mrecv[...])
    diagonal = (lax.broadcasted_iota(jnp.int32, (LANES, LANES), 0)
                == lax.broadcasted_iota(jnp.int32, (LANES, LANES), 1))
    for b in range(8):
        mass_ref[b:b + 1, :] = jnp.sum(
            jnp.where(diagonal, col_sum[LANES * b:LANES * (b + 1), :], 0.0), axis=0, keepdims=True)

    outs = []
    for b in range(2):
        lanes = slice(256 * b, 256 * (b + 1))
        product(core * 4 + 2 * b, own.at[b])
        partial_in[b].wait_recv()

        def finish(m, carry):
            rows = pl.ds(pl.multiple_of(m * 64, 64), 64)
            scale = 1.0 / (col_sum[rows, :] + PRIOR)
            total = own[b, rows, :] + nrecv[b, rows, :] + PRIOR * cent_ref[rows, lanes]
            fresh[rows, lanes] = total * jnp.concatenate([scale, scale], axis=1)
            return carry

        lax.fori_loop(0, CENTS // 64, finish, 0)
        out = pltpu.make_async_copy(fresh.at[:, lanes], out_ref.at[:, lanes], ls.at[2 + b])
        out.start()
        outs.append(out)

    for out in outs:
        out.wait()
    for copy in pending + partial_in + [mass_in]:
        copy.wait_send()


def per_device(points, centroids):
    vmem = pl.BlockSpec(memory_space=pltpu.VMEM)
    hbm = pl.BlockSpec(memory_space=pl.ANY)
    f32, bf16 = jnp.float32, jnp.bfloat16
    centers, mass = pl.pallas_call(
        kernel,
        out_shape=(jax.ShapeDtypeStruct((CENTS, HALF), f32), jax.ShapeDtypeStruct((8, LANES), f32)),
        in_specs=[hbm, hbm],
        out_specs=(hbm, vmem),
        scratch_shapes=[
            pltpu.VMEM((2 * ROWS, HALF), bf16),
            pltpu.VMEM((CENTS, HALF), f32),
            pltpu.VMEM((TILES, NZ, NX, NY, ROWS, LANES), bf16),
            pltpu.VMEM((4, ROWS, LANES), bf16),
            pltpu.VMEM((2, CENTS, HALF), bf16),
            pltpu.VMEM((CENTS, PTS), f32),
            pltpu.VMEM((CENTS, PTS), bf16),
            pltpu.VMEM((CENTS, LANES), f32),
            pltpu.VMEM((CENTS, LANES), f32),
            pltpu.VMEM((CENTS, LANES), f32),
            pltpu.VMEM((PBLOCKS, LANES), f32),
            pltpu.VMEM((ITERS, 8, LANES), f32),
            pltpu.VMEM((ITERS, 8, LANES), f32),
            pltpu.VMEM((ITERS, len(STAGES), PBLOCKS, LANES), f32),
            pltpu.VMEM((ITERS, STAGE_SEMS - 1, PBLOCKS, LANES), f32),
            pltpu.VMEM((8, LANES), f32),
            pltpu.VMEM((8, LANES), f32),
            pltpu.VMEM((2, CENTS, 256), f32),
            pltpu.VMEM((2, CENTS, 256), f32),
            pltpu.VMEM((2, CENTS, 256), f32),
            pltpu.VMEM((CENTS, HALF), f32),
            pltpu.SemaphoreType.DMA((GATHER_SEMS,)),
            pltpu.SemaphoreType.DMA((GATHER_SEMS,)),
            pltpu.SemaphoreType.DMA((ITERS, STAGE_SEMS)),
            pltpu.SemaphoreType.DMA((ITERS, STAGE_SEMS)),
            pltpu.SemaphoreType.DMA((3,)),
            pltpu.SemaphoreType.DMA((3,)),
            pltpu.SemaphoreType.DMA((4,)),
        ],
        compiler_params=pltpu.CompilerParams(
            collective_id=0, has_side_effects=True, vmem_limit_bytes=60 * 1024 * 1024),
    )(points, centroids)
    return centers, mass.reshape(CENTS)


def solution(mesh):
    return jax.shard_map(
        per_device,
        mesh=mesh,
        in_specs=(P("blk", "rep"), P("blk", "rep")),
        out_specs=(P("blk", "rep"), P("blk")),
        check_vma=False,
    )
```

```python
import math
from functools import reduce

import jax
import jax.numpy as jnp
from jax import lax
from jax.experimental import pallas as pl
from jax.experimental.pallas import tpu as pltpu
from jax.sharding import PartitionSpec as P

ITERS = 3
SCALE = 3.0
NZ, NX, NY = 8, 4, 4
CENTS = 1024
HALF = 512
ROWS = 16
PTS = NZ * NX * NY * ROWS
TILES = 8
LANES = 128
PBLOCKS = PTS // LANES
CGROUPS = CENTS // 8
LOG2_POINTS = 12.0
LOG2_CENTS = 17.0
PRIOR = 4096 / 131072
CHUNK = 256
MESH = pl.DeviceIdType.MESH
GATHER_SEMS = 148
PLANE = tuple((dx, dy) for dx in range(NX) for dy in range(NY) if dx or dy)
STAGES = ((0, len(PLANE)), (len(PLANE), NZ - 1))
STAGE_SEMS = len(PLANE) + NZ


def kernel(points_hbm, cent_hbm, out_ref, mass_ref, points_ref, cent_ref, pts, swap, cbf, logits, weights,
           col_max, col_sum, cpot, rpot, csend, crecv, rsend, rrecv, msend, mrecv, nsend, nrecv, own, fresh,
           gs, gr, its, itr, fs, fr, ls):
    blk = lax.axis_index("blk")
    core = lax.axis_index("rep")
    other = 1 - core
    z = lax.div(blk, NX * NY)
    x = lax.rem(lax.div(blk, NY), NX)
    y = lax.rem(blk, NY)

    def at(dz, dx, dy):
        return (lax.rem(z + dz, NZ) * (NX * NY) + lax.rem(x + dx, NX) * NY + lax.rem(y + dy, NY), core)

    sibling = (blk, other)

    points_in = pltpu.make_async_copy(points_hbm, points_ref, ls.at[0])
    points_in.start()
    own_in = pltpu.make_async_copy(cent_hbm, cent_ref, ls.at[1])
    own_in.start()
    barrier = pltpu.get_barrier_semaphore()
    pl.semaphore_signal(barrier, inc=1, device_id=sibling, device_id_type=MESH)
    for dx, dy in PLANE:
        pl.semaphore_signal(barrier, inc=1, device_id=at(0, dx, dy), device_id_type=MESH)
    for d in range(1, NZ):
        pl.semaphore_signal(barrier, inc=1, device_id=at(d, 0, 0), device_id_type=MESH)
    points_in.wait()
    for j in range(4):
        lanes = slice(LANES * j, LANES * (j + 1))
        swap[j] = points_ref[pl.ds(pl.multiple_of(other * ROWS, ROWS), ROWS), lanes]
        pts[core * 4 + j, z, x, y] = points_ref[pl.ds(pl.multiple_of(core * ROWS, ROWS), ROWS), lanes]
    pl.semaphore_wait(barrier, STAGE_SEMS)

    pending = []
    count = [0]

    def remote(src, dst, send_sem, recv_sem, device):
        copy = pltpu.make_async_remote_copy(
            src_ref=src, dst_ref=dst, send_sem=send_sem, recv_sem=recv_sem,
            device_id=device, device_id_type=MESH)
        copy.start()
        return copy

    def place(ref, device):
        q = count[0]
        count[0] += 1
        copy = remote(ref, ref, gs.at[q], gr.at[q], device)
        pending.append(copy)
        return copy

    count[0] += 1
    swapped = remote(swap, pts.at[pl.ds(core * 4, 4), z, x, y], gs.at[0], gr.at[0], sibling)
    pending.append(swapped)
    own_in.wait()
    cbf[core] = cent_ref[...].astype(jnp.bfloat16)
    cents_in = place(cbf.at[core], sibling)
    swapped.wait_recv()

    PZ, PX, PY, PXY = pl.ds(0, 2), pl.ds(2, 3), pl.ds(5, 3), pl.ds(2, 6)
    along_z = {}
    second, third, fourth = {}, {}, {}

    def spread_layer(dz):
        if dz:
            along_z[dz].wait_recv()
        layer = lax.rem(z + dz, NZ)
        second[dz] = []
        for d in (2, 1, 3):
            second[dz].append(place(pts.at[PX, layer, x, y], at(0, 0, d)))
            second[dz].append(place(pts.at[PY, layer, x, y], at(0, d, 0)))

    def x_line(dz, dx):
        return pts.at[PX, lax.rem(z + dz, NZ), lax.rem(x + dx, NX)]

    def y_line(dz, dy):
        return pts.at[PY, lax.rem(z + dz, NZ), :, lax.rem(y + dy, NY)]

    def send_lines(dz):
        for copy in second[dz]:
            copy.wait_recv()
        third[dz] = {}
        for d in (1, 3):
            third[dz]["x", d] = place(x_line(dz, 0), at(0, d, 0))
            third[dz]["y", d] = place(y_line(dz, 0), at(0, 0, d))

    def forward_lines(dz):
        d = 1 if dz % 2 else 3
        third[dz]["x", d].wait_recv()
        right = place(x_line(dz, NX - d), at(0, d, 0))
        third[dz]["y", d].wait_recv()
        fourth[dz] = (right, place(y_line(dz, NY - d), at(0, 0, d)))

    def layer_done(dz):
        d = 3 if dz % 2 else 1
        third[dz]["x", d].wait_recv()
        third[dz]["y", d].wait_recv()
        for copy in fourth[dz]:
            copy.wait_recv()

    def z_block(d, c):
        return pts.at[PZ, lax.rem(z + d, NZ), lax.rem(x + c, NX)]

    plane, up, down = {}, {}, {}

    def z_step(s, c):
        if s > 1:
            up[s - 1, c].wait_recv()
            down[s - 1, c].wait_recv()
        else:
            for copy in plane[c]:
                copy.wait_recv()
        if s < NZ // 2 or c < 2:
            up[s, c] = place(z_block(NZ - s + 1, c), at(1, 0, 0))
        if s < NZ // 2 or c >= 2:
            down[s, c] = place(z_block(s - 1, c), at(NZ - 1, 0, 0))

    for d in (1, 7, 2, 6, 3, 5, 4):
        along_z[NZ - d] = place(pts.at[PXY, z, x, y], at(d, 0, 0))
    spread_layer(0)
    for dx in (0, 2, 1, 3):
        plane[(NX - dx) % NX] = [place(pts.at[PZ, z, x, y], at(0, dx, dy)) for dy in range(NY) if dx or dy]

    def logit_block(dz):
        layer_done(dz)
        if dz == 0:
            cents_in.wait_recv()
        elif dz == NZ // 2:
            for copy in (up[dz, 0], up[dz, 1], down[dz, 2], down[dz, 3]):
                copy.wait_recv()
        layer = lax.rem(z + dz, NZ)
        lanes = pl.ds(pl.multiple_of(layer * 256, 256), 256)

        def part(m, carry):
            rows = pl.ds(pl.multiple_of(m * CHUNK, CHUNK), CHUNK)
            acc = None
            for h in range(2):
                block = jnp.concatenate(
                    [pts[4 * h + j, layer].reshape(NX * NY * ROWS, LANES) for j in range(4)], axis=1)
                term = lax.dot_general(
                    cbf[h, rows, :], block, (((1,), (1,)), ((), ())), preferred_element_type=jnp.float32)
                acc = term if acc is None else acc + term
            logits[rows, lanes] = acc * (SCALE * math.log2(math.e))
            return carry

        lax.fori_loop(0, CENTS // CHUNK, part, 0)

    tasks = {"a": spread_layer, "b": send_lines, "c": forward_lines, "r": z_step, "m": logit_block}
    for step in (
        ("a", 1), ("a", 7), ("b", 0), ("r", 1, 0), ("r", 1, 1), ("r", 1, 3), ("r", 1, 2), ("a", 2), ("a", 6), ("b", 1),
        ("b", 7), ("a", 3), ("a", 5), ("c", 0), ("r", 2, 0), ("r", 2, 1), ("r", 2, 3), ("r", 2, 2), ("a", 4), ("b", 2),
        ("b", 6), ("c", 1), ("c", 7), ("m", 0), ("b", 3), ("b", 5), ("r", 3, 0), ("r", 3, 1), ("r", 3, 3), ("r", 3, 2),
        ("c", 2), ("c", 6), ("m", 1), ("m", 7), ("b", 4), ("r", 4, 0), ("r", 4, 1), ("r", 4, 3), ("r", 4, 2), ("c", 3),
        ("c", 5), ("m", 2), ("m", 6), ("c", 4), ("m", 3), ("m", 5), ("m", 4),
    ):
        tasks[step[0]](*step[1:])

    lane = lax.broadcasted_iota(jnp.int32, (8, LANES), 1)

    def compact(column):
        acc = jnp.zeros((8, LANES), jnp.float32)
        for g in range(CGROUPS):
            acc = jnp.where(lane == g, jnp.broadcast_to(column[8 * g:8 * g + 8], (8, LANES)), acc)
        return acc

    def spread(dst, value):
        for g in range(CGROUPS):
            dst[8 * g:8 * g + 8, :] = jnp.broadcast_to(value[:, g:g + 1], (8, LANES))

    def merge(parts):
        top = reduce(jnp.maximum, parts)
        return top + jnp.log2(sum(jnp.exp2(p - top) for p in parts))

    def col_pass(h):
        def block(g, c):
            rows = pl.ds(pl.multiple_of(g * 32, 32), 32)
            vals = [logits[rows, LANES * j:LANES * (j + 1)] + rpot[j:j + 1, :] for j in range(8 * h, 8 * h + 8)]
            top = reduce(jnp.maximum, vals)
            if h:
                before = col_max[rows, :]
                top = jnp.maximum(top, before)
            total = sum(jnp.exp2(v - top) for v in vals)
            if h:
                total = total + col_sum[rows, :] * jnp.exp2(before - top)
            col_max[rows, :] = top
            col_sum[rows, :] = total
            return c

        lax.fori_loop(0, CENTS // 32, block, 0, unroll=4)

    def plan_pass(h):
        def block(g, c):
            rows = pl.ds(pl.multiple_of(g * 32, 32), 32)
            pot = cpot[rows, :] + LOG2_POINTS
            total = col_sum[rows, :] if h else None
            for j in range(8 * h, 8 * h + 8):
                lanes = slice(LANES * j, LANES * (j + 1))
                value = jnp.exp2(logits[rows, lanes] + rpot[j:j + 1, :] + pot)
                weights[rows, lanes] = value.astype(jnp.bfloat16)
                total = value if total is None else total + value
            col_sum[rows, :] = total
            return c

        lax.fori_loop(0, CENTS // 32, block, 0, unroll=4)

    def row_pass(it, h):
        for jb in (2 * h, 2 * h + 1):
            def row_block(q, carry):
                tops, sums = carry
                rows = pl.ds(pl.multiple_of(q * 64, 64), 64)
                pot = cpot[rows, :].reshape(8, 8, LANES)
                new_tops, new_sums = [], []
                for j in range(4):
                    lanes = slice(512 * jb + LANES * j, 512 * jb + LANES * (j + 1))
                    vals = logits[rows, lanes].reshape(8, 8, LANES) + pot
                    top = jnp.maximum(tops[j], jnp.max(vals, axis=0))
                    new_sums.append(sums[j] * jnp.exp2(tops[j] - top) + jnp.sum(jnp.exp2(vals - top[None]), axis=0))
                    new_tops.append(top)
                return tuple(new_tops), tuple(new_sums)

            low = tuple(jnp.full((8, LANES), -3e38, jnp.float32) for _ in range(4))
            none = tuple(jnp.zeros((8, LANES), jnp.float32) for _ in range(4))
            tops, sums = lax.fori_loop(0, CENTS // 64, row_block, (low, none), unroll=4)
            for j in range(4):
                top = jnp.max(tops[j], axis=0, keepdims=True)
                total = jnp.sum(sums[j] * jnp.exp2(tops[j] - top), axis=0, keepdims=True)
                row = 4 * (jb % 2) + j
                rsend[it, h, 0, row:row + 1, :] = top + jnp.log2(total)

    def start(it, h, k):
        base, _ = STAGES[k]
        peers = [at(0, dx, dy) for dx, dy in PLANE] if k == 0 else [at(d, 0, 0) for d in range(1, NZ)]
        return [remote(rsend.at[it, h, k], rrecv.at[it, h, base + q], its.at[it, h, base + q],
                       itr.at[it, h, base + q], peer) for q, peer in enumerate(peers)]

    def collect(it, h, k, copies):
        base, n = STAGES[k]
        for copy in copies:
            copy.wait_recv()
        return merge([rsend[it, h, k]] + [rrecv[it, h, base + q] for q in range(n)])

    def sweep(it, tail):
        top = jnp.max(col_max[...], axis=1, keepdims=True)
        total = jnp.sum(col_sum[...] * jnp.exp2(col_max[...] - top), axis=1, keepdims=True)
        mine = compact(top + jnp.log2(total))
        csend[it] = mine
        pair = remote(csend.at[it], crecv.at[it], its.at[it, 0, STAGE_SEMS - 1], itr.at[it, 0, STAGE_SEMS - 1],
                      sibling)
        pair.wait_recv()
        spread(cpot, -LOG2_CENTS - merge([mine, crecv[it]]))
        plane_out, z_out = [], []
        for h in range(2):
            row_pass(it, h)
            plane_out.append(start(it, h, 0))
        for h in range(2):
            rsend[it, h, 1] = collect(it, h, 0, plane_out[h])
            z_out.append(start(it, h, 1))
        for h in range(2):
            rpot[8 * h:8 * h + 8, :] = -LOG2_POINTS - collect(it, h, 1, z_out[h])
            tail(h)
        for copy in [pair] + plane_out[0] + plane_out[1] + z_out[0] + z_out[1]:
            copy.wait_send()

    rpot[...] = jnp.zeros((PBLOCKS, LANES), jnp.float32)
    col_pass(0)
    col_pass(1)

    def inner(it, carry):
        sweep(it, col_pass)
        return carry

    lax.fori_loop(0, ITERS - 1, inner, 0)
    sweep(ITERS - 1, plan_pass)

    mine = compact(jnp.sum(col_sum[...], axis=1, keepdims=True))
    msend[...] = mine
    mass_in = remote(msend, mrecv, fs.at[2], fr.at[2], sibling)

    def product(tile, dst):
        block = jnp.concatenate([pts[tile + j].reshape(PTS, LANES) for j in range(2)], axis=1)

        def part(m, carry):
            rows = pl.ds(pl.multiple_of(m * CHUNK, CHUNK), CHUNK)
            dst[rows, :] = jnp.dot(weights[rows, :], block, preferred_element_type=jnp.float32)
            return carry

        lax.fori_loop(0, CENTS // CHUNK, part, 0)

    partial_in = []
    for b in range(2):
        product(other * 4 + 2 * b, nsend.at[b])
        partial_in.append(remote(nsend.at[b], nrecv.at[b], fs.at[b], fr.at[b], sibling))

    mass_in.wait_recv()
    spread(col_sum, mine + mrecv[...])
    diagonal = (lax.broadcasted_iota(jnp.int32, (LANES, LANES), 0)
                == lax.broadcasted_iota(jnp.int32, (LANES, LANES), 1))
    for b in range(8):
        mass_ref[b:b + 1, :] = jnp.sum(
            jnp.where(diagonal, col_sum[LANES * b:LANES * (b + 1), :], 0.0), axis=0, keepdims=True)

    outs = []
    for b in range(2):
        lanes = slice(256 * b, 256 * (b + 1))
        product(core * 4 + 2 * b, own.at[b])
        partial_in[b].wait_recv()

        def finish(m, carry):
            rows = pl.ds(pl.multiple_of(m * 64, 64), 64)
            scale = 1.0 / (col_sum[rows, :] + PRIOR)
            total = own[b, rows, :] + nrecv[b, rows, :] + PRIOR * cent_ref[rows, lanes]
            fresh[rows, lanes] = total * jnp.concatenate([scale, scale], axis=1)
            return carry

        lax.fori_loop(0, CENTS // 64, finish, 0)
        out = pltpu.make_async_copy(fresh.at[:, lanes], out_ref.at[:, lanes], ls.at[2 + b])
        out.start()
        outs.append(out)

    for out in outs:
        out.wait()
    for copy in pending + partial_in + [mass_in]:
        copy.wait_send()


def per_device(points, centroids):
    vmem = pl.BlockSpec(memory_space=pltpu.VMEM)
    hbm = pl.BlockSpec(memory_space=pl.ANY)
    f32, bf16 = jnp.float32, jnp.bfloat16
    centers, mass = pl.pallas_call(
        kernel,
        out_shape=(jax.ShapeDtypeStruct((CENTS, HALF), f32), jax.ShapeDtypeStruct((8, LANES), f32)),
        in_specs=[hbm, hbm],
        out_specs=(hbm, vmem),
        scratch_shapes=[
            pltpu.VMEM((2 * ROWS, HALF), bf16),
            pltpu.VMEM((CENTS, HALF), f32),
            pltpu.VMEM((TILES, NZ, NX, NY, ROWS, LANES), bf16),
            pltpu.VMEM((4, ROWS, LANES), bf16),
            pltpu.VMEM((2, CENTS, HALF), bf16),
            pltpu.VMEM((CENTS, PTS), f32),
            pltpu.VMEM((CENTS, PTS), bf16),
            pltpu.VMEM((CENTS, LANES), f32),
            pltpu.VMEM((CENTS, LANES), f32),
            pltpu.VMEM((CENTS, LANES), f32),
            pltpu.VMEM((PBLOCKS, LANES), f32),
            pltpu.VMEM((ITERS, 8, LANES), f32),
            pltpu.VMEM((ITERS, 8, LANES), f32),
            pltpu.VMEM((ITERS, 2, len(STAGES), 8, LANES), f32),
            pltpu.VMEM((ITERS, 2, STAGE_SEMS - 1, 8, LANES), f32),
            pltpu.VMEM((8, LANES), f32),
            pltpu.VMEM((8, LANES), f32),
            pltpu.VMEM((2, CENTS, 256), f32),
            pltpu.VMEM((2, CENTS, 256), f32),
            pltpu.VMEM((2, CENTS, 256), f32),
            pltpu.VMEM((CENTS, HALF), f32),
            pltpu.SemaphoreType.DMA((GATHER_SEMS,)),
            pltpu.SemaphoreType.DMA((GATHER_SEMS,)),
            pltpu.SemaphoreType.DMA((ITERS, 2, STAGE_SEMS)),
            pltpu.SemaphoreType.DMA((ITERS, 2, STAGE_SEMS)),
            pltpu.SemaphoreType.DMA((3,)),
            pltpu.SemaphoreType.DMA((3,)),
            pltpu.SemaphoreType.DMA((4,)),
        ],
        compiler_params=pltpu.CompilerParams(
            collective_id=0, has_side_effects=True, vmem_limit_bytes=60 * 1024 * 1024),
    )(points, centroids)
    return centers, mass.reshape(CENTS)


def solution(mesh):
    return jax.shard_map(
        per_device,
        mesh=mesh,
        in_specs=(P("blk", "rep"), P("blk", "rep")),
        out_specs=(P("blk", "rep"), P("blk")),
        check_vma=False,
    )
```

```python
import math
from functools import reduce

import jax
import jax.numpy as jnp
from jax import lax
from jax.experimental import pallas as pl
from jax.experimental.pallas import tpu as pltpu
from jax.sharding import PartitionSpec as P

ITERS = 3
SCALE = 3.0
NZ, NX, NY = 8, 4, 4
CENTS = 1024
HALF = 512
ROWS = 16
PTS = NZ * NX * NY * ROWS
TILES = 8
LANES = 128
PBLOCKS = PTS // LANES
CGROUPS = CENTS // 8
LOG2_POINTS = 12.0
LOG2_CENTS = 17.0
PRIOR = 4096 / 131072
CHUNK = 256
BLOCK = 512
MESH = pl.DeviceIdType.MESH
GATHER_SEMS = 148
PLANE = tuple((dx, dy) for dx in range(NX) for dy in range(NY) if dx or dy)
STAGES = ((0, len(PLANE)), (len(PLANE), NZ - 1))
STAGE_SEMS = len(PLANE) + NZ


def kernel(points_hbm, cent_hbm, out_ref, mass_ref, spread_ref, points_ref, cent_ref, pts, swap, cbf, logits, weights,
           col_max, col_sum, cpot, rpot, csend, crecv, rsend, rrecv, msend, mrecv, nsend, nrecv, own, fresh,
           gs, gr, its, itr, fs, fr, ls):
    blk = lax.axis_index("blk")
    core = lax.axis_index("rep")
    other = 1 - core
    z = lax.div(blk, NX * NY)
    x = lax.rem(lax.div(blk, NY), NX)
    y = lax.rem(blk, NY)

    def at(dz, dx, dy):
        return (lax.rem(z + dz, NZ) * (NX * NY) + lax.rem(x + dx, NX) * NY + lax.rem(y + dy, NY), core)

    sibling = (blk, other)

    points_in = pltpu.make_async_copy(points_hbm, points_ref, ls.at[0])
    points_in.start()
    own_in = pltpu.make_async_copy(cent_hbm, cent_ref, ls.at[1])
    own_in.start()
    barrier = pltpu.get_barrier_semaphore()
    pl.semaphore_signal(barrier, inc=1, device_id=sibling, device_id_type=MESH)
    for dx, dy in PLANE:
        pl.semaphore_signal(barrier, inc=1, device_id=at(0, dx, dy), device_id_type=MESH)
    for d in range(1, NZ):
        pl.semaphore_signal(barrier, inc=1, device_id=at(d, 0, 0), device_id_type=MESH)
    points_in.wait()
    for j in range(4):
        lanes = slice(LANES * j, LANES * (j + 1))
        swap[j] = points_ref[pl.ds(pl.multiple_of(other * ROWS, ROWS), ROWS), lanes]
        pts[core * 4 + j, z, x, y] = points_ref[pl.ds(pl.multiple_of(core * ROWS, ROWS), ROWS), lanes]
    pl.semaphore_wait(barrier, STAGE_SEMS)

    pending = []
    count = [0]

    def remote(src, dst, send_sem, recv_sem, device):
        copy = pltpu.make_async_remote_copy(
            src_ref=src, dst_ref=dst, send_sem=send_sem, recv_sem=recv_sem,
            device_id=device, device_id_type=MESH)
        copy.start()
        return copy

    def place(ref, device):
        q = count[0]
        count[0] += 1
        copy = remote(ref, ref, gs.at[q], gr.at[q], device)
        pending.append(copy)
        return copy

    count[0] += 1
    swapped = remote(swap, pts.at[pl.ds(core * 4, 4), z, x, y], gs.at[0], gr.at[0], sibling)
    pending.append(swapped)
    own_in.wait()
    cbf[core] = cent_ref[...].astype(jnp.bfloat16)
    cents_in = place(cbf.at[core], sibling)
    swapped.wait_recv()

    PZ, PX, PY, PXY = pl.ds(0, 2), pl.ds(2, 3), pl.ds(5, 3), pl.ds(2, 6)
    along_z = {}
    second, third, fourth = {}, {}, {}

    def spread_layer(dz):
        if dz:
            along_z[dz].wait_recv()
        layer = lax.rem(z + dz, NZ)
        second[dz] = []
        for d in (2, 1, 3):
            second[dz].append(place(pts.at[PX, layer, x, y], at(0, 0, d)))
            second[dz].append(place(pts.at[PY, layer, x, y], at(0, d, 0)))

    def x_line(dz, dx):
        return pts.at[PX, lax.rem(z + dz, NZ), lax.rem(x + dx, NX)]

    def y_line(dz, dy):
        return pts.at[PY, lax.rem(z + dz, NZ), :, lax.rem(y + dy, NY)]

    def send_lines(dz):
        for copy in second[dz]:
            copy.wait_recv()
        third[dz] = {}
        for d in (1, 3):
            third[dz]["x", d] = place(x_line(dz, 0), at(0, d, 0))
            third[dz]["y", d] = place(y_line(dz, 0), at(0, 0, d))

    def forward_lines(dz):
        d = 1 if dz % 2 else 3
        third[dz]["x", d].wait_recv()
        right = place(x_line(dz, NX - d), at(0, d, 0))
        third[dz]["y", d].wait_recv()
        fourth[dz] = (right, place(y_line(dz, NY - d), at(0, 0, d)))

    def layer_done(dz):
        d = 3 if dz % 2 else 1
        third[dz]["x", d].wait_recv()
        third[dz]["y", d].wait_recv()
        for copy in fourth[dz]:
            copy.wait_recv()

    def z_block(d, c):
        return pts.at[PZ, lax.rem(z + d, NZ), lax.rem(x + c, NX)]

    plane, up, down = {}, {}, {}

    def z_step(s, c):
        if s > 1:
            up[s - 1, c].wait_recv()
            down[s - 1, c].wait_recv()
        else:
            for copy in plane[c]:
                copy.wait_recv()
        if s < NZ // 2 or c < 2:
            up[s, c] = place(z_block(NZ - s + 1, c), at(1, 0, 0))
        if s < NZ // 2 or c >= 2:
            down[s, c] = place(z_block(s - 1, c), at(NZ - 1, 0, 0))

    for d in (1, 7, 2, 6, 3, 5, 4):
        along_z[NZ - d] = place(pts.at[PXY, z, x, y], at(d, 0, 0))
    spread_layer(0)
    for dx in (0, 2, 1, 3):
        plane[(NX - dx) % NX] = [place(pts.at[PZ, z, x, y], at(0, dx, dy)) for dy in range(NY) if dx or dy]

    def logit_block(dz):
        layer_done(dz)
        if dz == 0:
            cents_in.wait_recv()
        elif dz == NZ // 2:
            for copy in (up[dz, 0], up[dz, 1], down[dz, 2], down[dz, 3]):
                copy.wait_recv()
        layer = lax.rem(z + dz, NZ)
        lanes = pl.ds(pl.multiple_of(layer * 256, 256), 256)

        def part(m, carry):
            rows = pl.ds(pl.multiple_of(m * CHUNK, CHUNK), CHUNK)
            acc = None
            for h in range(2):
                block = jnp.concatenate(
                    [pts[4 * h + j, layer].reshape(NX * NY * ROWS, LANES) for j in range(4)], axis=1)
                term = lax.dot_general(
                    cbf[h, rows, :], block, (((1,), (1,)), ((), ())), preferred_element_type=jnp.float32)
                acc = term if acc is None else acc + term
            logits[rows, lanes] = acc * (SCALE * math.log2(math.e))
            return carry

        lax.fori_loop(0, CENTS // CHUNK, part, 0)

    tasks = {"a": spread_layer, "b": send_lines, "c": forward_lines, "r": z_step, "m": logit_block}
    for step in (
        ("a", 1), ("a", 7), ("b", 0), ("r", 1, 0), ("r", 1, 1), ("r", 1, 3), ("r", 1, 2), ("a", 2), ("a", 6), ("b", 1),
        ("b", 7), ("a", 3), ("a", 5), ("c", 0), ("r", 2, 0), ("r", 2, 1), ("r", 2, 3), ("r", 2, 2), ("a", 4), ("b", 2),
        ("b", 6), ("c", 1), ("c", 7), ("m", 0), ("b", 3), ("b", 5), ("r", 3, 0), ("r", 3, 1), ("r", 3, 3), ("r", 3, 2),
        ("c", 2), ("c", 6), ("m", 1), ("m", 7), ("b", 4), ("r", 4, 0), ("r", 4, 1), ("r", 4, 3), ("r", 4, 2), ("c", 3),
        ("c", 5), ("m", 2), ("m", 6), ("c", 4), ("m", 3), ("m", 5), ("m", 4),
    ):
        tasks[step[0]](*step[1:])

    lane = lax.broadcasted_iota(jnp.int32, (8, LANES), 1)

    def compact(column):
        acc = jnp.zeros((8, LANES), jnp.float32)
        for g in range(CGROUPS):
            acc = jnp.where(lane == g, jnp.broadcast_to(column[8 * g:8 * g + 8], (8, LANES)), acc)
        return acc

    def spread(dst, value):
        for g in range(CGROUPS):
            dst[8 * g:8 * g + 8, :] = jnp.broadcast_to(value[:, g:g + 1], (8, LANES))

    def merge(parts):
        top = reduce(jnp.maximum, parts)
        return top + jnp.log2(sum(jnp.exp2(p - top) for p in parts))

    def col_pass(h):
        def block(g, c):
            rows = pl.ds(pl.multiple_of(g * 32, 32), 32)
            vals = [logits[rows, LANES * j:LANES * (j + 1)] + rpot[j:j + 1, :] for j in range(8 * h, 8 * h + 8)]
            top = reduce(jnp.maximum, vals)
            if h:
                before = col_max[rows, :]
                top = jnp.maximum(top, before)
            total = sum(jnp.exp2(v - top) for v in vals)
            if h:
                total = total + col_sum[rows, :] * jnp.exp2(before - top)
            col_max[rows, :] = top
            col_sum[rows, :] = total
            return c

        lax.fori_loop(0, CENTS // 32, block, 0, unroll=4)

    def plan_pass(h):
        def block(g, c):
            rows = pl.ds(pl.multiple_of(g * 32, 32), 32)
            pot = cpot[rows, :] + LOG2_POINTS
            total = col_sum[rows, :] if h else None
            for j in range(8 * h, 8 * h + 8):
                lanes = slice(LANES * j, LANES * (j + 1))
                value = jnp.exp2(logits[rows, lanes] + rpot[j:j + 1, :] + pot)
                weights[rows, lanes] = value.astype(jnp.bfloat16)
                total = value if total is None else total + value
            col_sum[rows, :] = total
            return c

        lax.fori_loop(0, CENTS // 32, block, 0, unroll=4)

    def row_pass(it, h):
        for jb in (2 * h, 2 * h + 1):
            def row_block(q, carry):
                tops, sums = carry
                rows = pl.ds(pl.multiple_of(q * 64, 64), 64)
                pot = cpot[rows, :].reshape(8, 8, LANES)
                new_tops, new_sums = [], []
                for j in range(4):
                    lanes = slice(512 * jb + LANES * j, 512 * jb + LANES * (j + 1))
                    vals = logits[rows, lanes].reshape(8, 8, LANES) + pot
                    top = jnp.maximum(tops[j], jnp.max(vals, axis=0))
                    new_sums.append(sums[j] * jnp.exp2(tops[j] - top) + jnp.sum(jnp.exp2(vals - top[None]), axis=0))
                    new_tops.append(top)
                return tuple(new_tops), tuple(new_sums)

            low = tuple(jnp.full((8, LANES), -3e38, jnp.float32) for _ in range(4))
            none = tuple(jnp.zeros((8, LANES), jnp.float32) for _ in range(4))
            tops, sums = lax.fori_loop(0, CENTS // 64, row_block, (low, none), unroll=4)
            for j in range(4):
                top = jnp.max(tops[j], axis=0, keepdims=True)
                total = jnp.sum(sums[j] * jnp.exp2(tops[j] - top), axis=0, keepdims=True)
                row = 4 * (jb % 2) + j
                rsend[it, h, 0, row:row + 1, :] = top + jnp.log2(total)

    def start(it, h, k):
        base, _ = STAGES[k]
        peers = [at(0, dx, dy) for dx, dy in PLANE] if k == 0 else [at(d, 0, 0) for d in range(1, NZ)]
        return [remote(rsend.at[it, h, k], rrecv.at[it, h, base + q], its.at[it, h, base + q],
                       itr.at[it, h, base + q], peer) for q, peer in enumerate(peers)]

    def collect(it, h, k, copies):
        base, n = STAGES[k]
        for copy in copies:
            copy.wait_recv()
        return merge([rsend[it, h, k]] + [rrecv[it, h, base + q] for q in range(n)])

    def sweep(it, tail):
        top = jnp.max(col_max[...], axis=1, keepdims=True)
        total = jnp.sum(col_sum[...] * jnp.exp2(col_max[...] - top), axis=1, keepdims=True)
        mine = compact(top + jnp.log2(total))
        csend[it] = mine
        pair = remote(csend.at[it], crecv.at[it], its.at[it, 0, STAGE_SEMS - 1], itr.at[it, 0, STAGE_SEMS - 1],
                      sibling)
        pair.wait_recv()
        spread(cpot, -LOG2_CENTS - merge([mine, crecv[it]]))
        plane_out, z_out = [], []
        for h in range(2):
            row_pass(it, h)
            plane_out.append(start(it, h, 0))
        for h in range(2):
            rsend[it, h, 1] = collect(it, h, 0, plane_out[h])
            z_out.append(start(it, h, 1))
        for h in range(2):
            rpot[8 * h:8 * h + 8, :] = -LOG2_POINTS - collect(it, h, 1, z_out[h])
            tail(h)
        for copy in [pair] + plane_out[0] + plane_out[1] + z_out[0] + z_out[1]:
            copy.wait_send()

    rpot[...] = jnp.zeros((PBLOCKS, LANES), jnp.float32)
    col_pass(0)
    col_pass(1)

    def inner(it, carry):
        sweep(it, col_pass)
        return carry

    lax.fori_loop(0, ITERS - 1, inner, 0)
    sweep(ITERS - 1, plan_pass)

    mine = compact(jnp.sum(col_sum[...], axis=1, keepdims=True))
    msend[...] = mine
    mass_in = remote(msend, mrecv, fs.at[2], fr.at[2], sibling)

    def product(tile, dst):
        block = jnp.concatenate([pts[tile + j].reshape(PTS, LANES) for j in range(2)], axis=1)

        def part(m, carry):
            rows = pl.ds(pl.multiple_of(m * CHUNK, CHUNK), CHUNK)
            dst[rows, :] = jnp.dot(weights[rows, :], block, preferred_element_type=jnp.float32)
            return carry

        lax.fori_loop(0, CENTS // CHUNK, part, 0)

    partial_in = []
    for b in range(2):
        product(other * 4 + 2 * b, nsend.at[b])
        partial_in.append(remote(nsend.at[b], nrecv.at[b], fs.at[b], fr.at[b], sibling))

    mass_in.wait_recv()
    spread(col_sum, mine + mrecv[...])
    masses_out = pltpu.make_async_copy(col_sum, spread_ref, ls.at[4])
    masses_out.start()
    diagonal = (lax.broadcasted_iota(jnp.int32, (LANES, LANES), 0)
                == lax.broadcasted_iota(jnp.int32, (LANES, LANES), 1))
    for b in range(8):
        mass_ref[b:b + 1, :] = jnp.sum(
            jnp.where(diagonal, col_sum[LANES * b:LANES * (b + 1), :], 0.0), axis=0, keepdims=True)

    outs = [masses_out]
    for b in range(2):
        lanes = slice(256 * b, 256 * (b + 1))
        product(core * 4 + 2 * b, own.at[b])
        partial_in[b].wait_recv()

        def finish(m, carry):
            rows = pl.ds(pl.multiple_of(m * 64, 64), 64)
            fresh[rows, lanes] = own[b, rows, :] + nrecv[b, rows, :] + PRIOR * cent_ref[rows, lanes]
            return carry

        lax.fori_loop(0, CENTS // 64, finish, 0)
        out = pltpu.make_async_copy(fresh.at[:, lanes], out_ref.at[:, lanes], ls.at[2 + b])
        out.start()
        outs.append(out)

    for out in outs:
        out.wait()
    for copy in pending + partial_in + [mass_in]:
        copy.wait_send()


def divide(total_ref, spread_ref, mass_ref, out_ref, mass_out):
    scale = 1.0 / (spread_ref[...] + PRIOR)
    mass_out[...] = mass_ref[...]
    out_ref[...] = total_ref[...] * jnp.concatenate([scale] * (HALF // LANES), axis=1)


def per_device(points, centroids):
    vmem = pl.BlockSpec(memory_space=pltpu.VMEM)
    hbm = pl.BlockSpec(memory_space=pl.ANY)
    f32, bf16 = jnp.float32, jnp.bfloat16
    total, mass, masses = pl.pallas_call(
        kernel,
        out_shape=(jax.ShapeDtypeStruct((CENTS, HALF), f32), jax.ShapeDtypeStruct((8, LANES), f32),
                   jax.ShapeDtypeStruct((CENTS, LANES), f32)),
        in_specs=[hbm, hbm],
        out_specs=(hbm, vmem, hbm),
        scratch_shapes=[
            pltpu.VMEM((2 * ROWS, HALF), bf16),
            pltpu.VMEM((CENTS, HALF), f32),
            pltpu.VMEM((TILES, NZ, NX, NY, ROWS, LANES), bf16),
            pltpu.VMEM((4, ROWS, LANES), bf16),
            pltpu.VMEM((2, CENTS, HALF), bf16),
            pltpu.VMEM((CENTS, PTS), f32),
            pltpu.VMEM((CENTS, PTS), bf16),
            pltpu.VMEM((CENTS, LANES), f32),
            pltpu.VMEM((CENTS, LANES), f32),
            pltpu.VMEM((CENTS, LANES), f32),
            pltpu.VMEM((PBLOCKS, LANES), f32),
            pltpu.VMEM((ITERS, 8, LANES), f32),
            pltpu.VMEM((ITERS, 8, LANES), f32),
            pltpu.VMEM((ITERS, 2, len(STAGES), 8, LANES), f32),
            pltpu.VMEM((ITERS, 2, STAGE_SEMS - 1, 8, LANES), f32),
            pltpu.VMEM((8, LANES), f32),
            pltpu.VMEM((8, LANES), f32),
            pltpu.VMEM((2, CENTS, 256), f32),
            pltpu.VMEM((2, CENTS, 256), f32),
            pltpu.VMEM((2, CENTS, 256), f32),
            pltpu.VMEM((CENTS, HALF), f32),
            pltpu.SemaphoreType.DMA((GATHER_SEMS,)),
            pltpu.SemaphoreType.DMA((GATHER_SEMS,)),
            pltpu.SemaphoreType.DMA((ITERS, 2, STAGE_SEMS)),
            pltpu.SemaphoreType.DMA((ITERS, 2, STAGE_SEMS)),
            pltpu.SemaphoreType.DMA((3,)),
            pltpu.SemaphoreType.DMA((3,)),
            pltpu.SemaphoreType.DMA((5,)),
        ],
        compiler_params=pltpu.CompilerParams(
            collective_id=0, has_side_effects=True, vmem_limit_bytes=60 * 1024 * 1024),
    )(points, centroids)
    centers, mass = pl.pallas_call(
        divide,
        out_shape=(jax.ShapeDtypeStruct((CENTS, HALF), f32), jax.ShapeDtypeStruct((8, LANES), f32)),
        grid=(CENTS // BLOCK,),
        in_specs=[pl.BlockSpec((BLOCK, HALF), lambda i: (i, 0)), pl.BlockSpec((BLOCK, LANES), lambda i: (i, 0)),
                  pl.BlockSpec((8, LANES), lambda i: (0, 0))],
        out_specs=(pl.BlockSpec((BLOCK, HALF), lambda i: (i, 0)), pl.BlockSpec((8, LANES), lambda i: (0, 0))),
    )(total, masses, mass)
    return centers, mass.reshape(CENTS)


def solution(mesh):
    return jax.shard_map(
        per_device,
        mesh=mesh,
        in_specs=(P("blk", "rep"), P("blk", "rep")),
        out_specs=(P("blk", "rep"), P("blk")),
        check_vma=False,
    )
```

```python
import math
from functools import reduce

import jax
import jax.numpy as jnp
from jax import lax
from jax.experimental import pallas as pl
from jax.experimental.pallas import tpu as pltpu
from jax.sharding import PartitionSpec as P

ITERS = 3
SCALE = 3.0
NZ, NX, NY = 8, 4, 4
CENTS = 1024
HALF = 512
ROWS = 16
PTS = NZ * NX * NY * ROWS
TILES = 8
LANES = 128
PBLOCKS = PTS // LANES
CGROUPS = CENTS // 8
LOG2_POINTS = 12.0
LOG2_CENTS = 17.0
PRIOR = 4096 / 131072
CHUNK = 512
BLOCK = 512
MESH = pl.DeviceIdType.MESH
GATHER_SEMS = 148
PLANE = tuple(sorted(((dx, dy) for dx in range(NX) for dy in range(NY) if dx or dy),
                     key=lambda d: -min(d[0], NX - d[0]) - min(d[1], NY - d[1])))
LAYERS = (4, 3, 5, 2, 6, 1, 7)
STAGES = ((0, len(PLANE)), (len(PLANE), NZ - 1))
STAGE_SEMS = len(PLANE) + NZ


def kernel(points_hbm, cent_hbm, out_ref, mass_ref, spread_ref, points_ref, cent_ref, pts, swap, cbf, logits, weights,
           col_max, col_sum, cpot, rpot, csend, crecv, rsend, rrecv, msend, mrecv, nsend, nrecv, own, fresh,
           gs, gr, its, itr, fs, fr, ls):
    blk = lax.axis_index("blk")
    core = lax.axis_index("rep")
    other = 1 - core
    z = lax.div(blk, NX * NY)
    x = lax.rem(lax.div(blk, NY), NX)
    y = lax.rem(blk, NY)

    def at(dz, dx, dy):
        return (lax.rem(z + dz, NZ) * (NX * NY) + lax.rem(x + dx, NX) * NY + lax.rem(y + dy, NY), core)

    sibling = (blk, other)

    points_in = pltpu.make_async_copy(points_hbm, points_ref, ls.at[0])
    points_in.start()
    own_in = pltpu.make_async_copy(cent_hbm, cent_ref, ls.at[1])
    own_in.start()
    barrier = pltpu.get_barrier_semaphore()
    pl.semaphore_signal(barrier, inc=1, device_id=sibling, device_id_type=MESH)
    for dx, dy in PLANE:
        pl.semaphore_signal(barrier, inc=1, device_id=at(0, dx, dy), device_id_type=MESH)
    for d in range(1, NZ):
        pl.semaphore_signal(barrier, inc=1, device_id=at(d, 0, 0), device_id_type=MESH)
    points_in.wait()
    for j in range(4):
        lanes = slice(LANES * j, LANES * (j + 1))
        swap[j] = points_ref[pl.ds(pl.multiple_of(other * ROWS, ROWS), ROWS), lanes]
        pts[core * 4 + j, z, x, y] = points_ref[pl.ds(pl.multiple_of(core * ROWS, ROWS), ROWS), lanes]
    pl.semaphore_wait(barrier, STAGE_SEMS)

    pending = []
    count = [0]

    def remote(src, dst, send_sem, recv_sem, device):
        copy = pltpu.make_async_remote_copy(
            src_ref=src, dst_ref=dst, send_sem=send_sem, recv_sem=recv_sem,
            device_id=device, device_id_type=MESH)
        copy.start()
        return copy

    def place(ref, device):
        q = count[0]
        count[0] += 1
        copy = remote(ref, ref, gs.at[q], gr.at[q], device)
        pending.append(copy)
        return copy

    count[0] += 1
    swapped = remote(swap, pts.at[pl.ds(core * 4, 4), z, x, y], gs.at[0], gr.at[0], sibling)
    pending.append(swapped)
    own_in.wait()
    cbf[core] = cent_ref[...].astype(jnp.bfloat16)
    cents_in = place(cbf.at[core], sibling)
    swapped.wait_recv()

    PZ, PX, PY, PXY = pl.ds(0, 2), pl.ds(2, 3), pl.ds(5, 3), pl.ds(2, 6)
    along_z = {}
    second, third, fourth = {}, {}, {}

    def spread_layer(dz):
        if dz:
            along_z[dz].wait_recv()
        layer = lax.rem(z + dz, NZ)
        second[dz] = []
        for d in (2, 1, 3):
            second[dz].append(place(pts.at[PX, layer, x, y], at(0, 0, d)))
            second[dz].append(place(pts.at[PY, layer, x, y], at(0, d, 0)))

    def x_line(dz, dx):
        return pts.at[PX, lax.rem(z + dz, NZ), lax.rem(x + dx, NX)]

    def y_line(dz, dy):
        return pts.at[PY, lax.rem(z + dz, NZ), :, lax.rem(y + dy, NY)]

    def send_lines(dz):
        for copy in second[dz]:
            copy.wait_recv()
        third[dz] = {}
        for d in (1, 3):
            third[dz]["x", d] = place(x_line(dz, 0), at(0, d, 0))
            third[dz]["y", d] = place(y_line(dz, 0), at(0, 0, d))

    def forward_lines(dz):
        d = 1 if dz % 2 else 3
        third[dz]["x", d].wait_recv()
        right = place(x_line(dz, NX - d), at(0, d, 0))
        third[dz]["y", d].wait_recv()
        fourth[dz] = (right, place(y_line(dz, NY - d), at(0, 0, d)))

    def layer_done(dz):
        d = 3 if dz % 2 else 1
        third[dz]["x", d].wait_recv()
        third[dz]["y", d].wait_recv()
        for copy in fourth[dz]:
            copy.wait_recv()

    def z_block(d, c):
        return pts.at[PZ, lax.rem(z + d, NZ), lax.rem(x + c, NX)]

    plane, up, down = {}, {}, {}

    def z_step(s, c):
        if s > 1:
            up[s - 1, c].wait_recv()
            down[s - 1, c].wait_recv()
        else:
            for copy in plane[c]:
                copy.wait_recv()
        if s < NZ // 2 or c < 2:
            up[s, c] = place(z_block(NZ - s + 1, c), at(1, 0, 0))
        if s < NZ // 2 or c >= 2:
            down[s, c] = place(z_block(s - 1, c), at(NZ - 1, 0, 0))

    for d in (1, 7, 2, 6, 3, 5, 4):
        along_z[NZ - d] = place(pts.at[PXY, z, x, y], at(d, 0, 0))
    spread_layer(0)
    for dx in (0, 2, 1, 3):
        plane[(NX - dx) % NX] = [place(pts.at[PZ, z, x, y], at(0, dx, dy)) for dy in range(NY) if dx or dy]

    def logit_block(dz):
        layer_done(dz)
        if dz == 0:
            cents_in.wait_recv()
        elif dz == NZ // 2:
            for copy in (up[dz, 0], up[dz, 1], down[dz, 2], down[dz, 3]):
                copy.wait_recv()
        layer = lax.rem(z + dz, NZ)
        lanes = pl.ds(pl.multiple_of(layer * 256, 256), 256)

        def part(m, carry):
            rows = pl.ds(pl.multiple_of(m * CHUNK, CHUNK), CHUNK)
            acc = None
            for h in range(2):
                block = jnp.concatenate(
                    [pts[4 * h + j, layer].reshape(NX * NY * ROWS, LANES) for j in range(4)], axis=1)
                term = lax.dot_general(
                    cbf[h, rows, :], block, (((1,), (1,)), ((), ())), preferred_element_type=jnp.float32)
                acc = term if acc is None else acc + term
            logits[rows, lanes] = acc * (SCALE * math.log2(math.e))
            return carry

        lax.fori_loop(0, CENTS // CHUNK, part, 0)

    tasks = {"a": spread_layer, "b": send_lines, "c": forward_lines, "r": z_step, "m": logit_block}
    for step in (
        ("a", 1), ("a", 7), ("b", 0), ("r", 1, 0), ("r", 1, 1), ("r", 1, 3), ("r", 1, 2), ("a", 2), ("a", 6), ("b", 1),
        ("b", 7), ("a", 3), ("a", 5), ("c", 0), ("r", 2, 0), ("r", 2, 1), ("r", 2, 3), ("r", 2, 2), ("a", 4), ("b", 2),
        ("b", 6), ("c", 1), ("c", 7), ("m", 0), ("b", 3), ("b", 5), ("r", 3, 0), ("r", 3, 1), ("r", 3, 3), ("r", 3, 2),
        ("c", 2), ("c", 6), ("m", 1), ("m", 7), ("b", 4), ("r", 4, 0), ("r", 4, 1), ("r", 4, 3), ("r", 4, 2), ("c", 3),
        ("c", 5), ("m", 2), ("m", 6), ("c", 4), ("m", 3), ("m", 5), ("m", 4),
    ):
        tasks[step[0]](*step[1:])

    lane = lax.broadcasted_iota(jnp.int32, (8, LANES), 1)

    def compact(column):
        acc = jnp.zeros((8, LANES), jnp.float32)
        for g in range(CGROUPS):
            acc = jnp.where(lane == g, jnp.broadcast_to(column[8 * g:8 * g + 8], (8, LANES)), acc)
        return acc

    def spread(dst, value):
        for g in range(CGROUPS):
            dst[8 * g:8 * g + 8, :] = jnp.broadcast_to(value[:, g:g + 1], (8, LANES))

    def merge(parts):
        top = reduce(jnp.maximum, parts)
        return top + jnp.log2(sum(jnp.exp2(p - top) for p in parts))

    def col_pass(h):
        def block(g, c):
            rows = pl.ds(pl.multiple_of(g * 32, 32), 32)
            vals = [logits[rows, LANES * j:LANES * (j + 1)] + rpot[j:j + 1, :] for j in range(8 * h, 8 * h + 8)]
            top = reduce(jnp.maximum, vals)
            if h:
                before = col_max[rows, :]
                top = jnp.maximum(top, before)
            total = sum(jnp.exp2(v - top) for v in vals)
            if h:
                total = total + col_sum[rows, :] * jnp.exp2(before - top)
            col_max[rows, :] = top
            col_sum[rows, :] = total
            return c

        lax.fori_loop(0, CENTS // 32, block, 0, unroll=4)

    def plan_pass(h):
        def block(g, c):
            rows = pl.ds(pl.multiple_of(g * 32, 32), 32)
            pot = cpot[rows, :] + LOG2_POINTS
            total = col_sum[rows, :] if h else None
            for j in range(8 * h, 8 * h + 8):
                lanes = slice(LANES * j, LANES * (j + 1))
                value = jnp.exp2(logits[rows, lanes] + rpot[j:j + 1, :] + pot)
                weights[rows, lanes] = value.astype(jnp.bfloat16)
                total = value if total is None else total + value
            col_sum[rows, :] = total
            return c

        lax.fori_loop(0, CENTS // 32, block, 0, unroll=4)

    def row_pass(it, h):
        for jb in (2 * h, 2 * h + 1):
            def row_block(q, carry):
                tops, sums = carry
                rows = pl.ds(pl.multiple_of(q * 64, 64), 64)
                pot = cpot[rows, :].reshape(8, 8, LANES)
                new_tops, new_sums = [], []
                for j in range(4):
                    lanes = slice(512 * jb + LANES * j, 512 * jb + LANES * (j + 1))
                    vals = logits[rows, lanes].reshape(8, 8, LANES) + pot
                    top = jnp.maximum(tops[j], jnp.max(vals, axis=0))
                    new_sums.append(sums[j] * jnp.exp2(tops[j] - top) + jnp.sum(jnp.exp2(vals - top[None]), axis=0))
                    new_tops.append(top)
                return tuple(new_tops), tuple(new_sums)

            low = tuple(jnp.full((8, LANES), -3e38, jnp.float32) for _ in range(4))
            none = tuple(jnp.zeros((8, LANES), jnp.float32) for _ in range(4))
            tops, sums = lax.fori_loop(0, CENTS // 64, row_block, (low, none), unroll=4)
            for j in range(4):
                top = jnp.max(tops[j], axis=0, keepdims=True)
                total = jnp.sum(sums[j] * jnp.exp2(tops[j] - top), axis=0, keepdims=True)
                row = 4 * (jb % 2) + j
                rsend[it, h, 0, row:row + 1, :] = top + jnp.log2(total)

    def start(it, h, k):
        base, _ = STAGES[k]
        peers = [at(0, dx, dy) for dx, dy in PLANE] if k == 0 else [at(d, 0, 0) for d in LAYERS]
        return [remote(rsend.at[it, h, k], rrecv.at[it, h, base + q], its.at[it, h, base + q],
                       itr.at[it, h, base + q], peer) for q, peer in enumerate(peers)]

    def collect(it, h, k, copies):
        base, n = STAGES[k]
        for copy in copies:
            copy.wait_recv()
        return merge([rsend[it, h, k]] + [rrecv[it, h, base + q] for q in range(n)])

    def sweep(it, tail):
        top = jnp.max(col_max[...], axis=1, keepdims=True)
        total = jnp.sum(col_sum[...] * jnp.exp2(col_max[...] - top), axis=1, keepdims=True)
        mine = compact(top + jnp.log2(total))
        csend[it] = mine
        pair = remote(csend.at[it], crecv.at[it], its.at[it, 0, STAGE_SEMS - 1], itr.at[it, 0, STAGE_SEMS - 1],
                      sibling)
        pair.wait_recv()
        spread(cpot, -LOG2_CENTS - merge([mine, crecv[it]]))
        plane_out, z_out = [], []
        for h in range(2):
            row_pass(it, h)
            plane_out.append(start(it, h, 0))
        for h in range(2):
            rsend[it, h, 1] = collect(it, h, 0, plane_out[h])
            z_out.append(start(it, h, 1))
        for h in range(2):
            rpot[8 * h:8 * h + 8, :] = -LOG2_POINTS - collect(it, h, 1, z_out[h])
            tail(h)
        for copy in [pair] + plane_out[0] + plane_out[1] + z_out[0] + z_out[1]:
            copy.wait_send()

    rpot[...] = jnp.zeros((PBLOCKS, LANES), jnp.float32)
    col_pass(0)
    col_pass(1)

    def inner(it, carry):
        sweep(it, col_pass)
        return carry

    lax.fori_loop(0, ITERS - 1, inner, 0)
    sweep(ITERS - 1, plan_pass)

    mine = compact(jnp.sum(col_sum[...], axis=1, keepdims=True))
    msend[...] = mine
    mass_in = remote(msend, mrecv, fs.at[2], fr.at[2], sibling)

    def product(tile, dst):
        block = jnp.concatenate([pts[tile + j].reshape(PTS, LANES) for j in range(2)], axis=1)

        def part(m, carry):
            rows = pl.ds(pl.multiple_of(m * CHUNK, CHUNK), CHUNK)
            dst[rows, :] = jnp.dot(weights[rows, :], block, preferred_element_type=jnp.float32)
            return carry

        lax.fori_loop(0, CENTS // CHUNK, part, 0)

    partial_in = []
    for b in range(2):
        product(other * 4 + 2 * b, nsend.at[b])
        partial_in.append(remote(nsend.at[b], nrecv.at[b], fs.at[b], fr.at[b], sibling))

    mass_in.wait_recv()
    spread(col_sum, mine + mrecv[...])
    masses_out = pltpu.make_async_copy(col_sum, spread_ref, ls.at[4])
    masses_out.start()
    diagonal = (lax.broadcasted_iota(jnp.int32, (LANES, LANES), 0)
                == lax.broadcasted_iota(jnp.int32, (LANES, LANES), 1))
    for b in range(8):
        mass_ref[b:b + 1, :] = jnp.sum(
            jnp.where(diagonal, col_sum[LANES * b:LANES * (b + 1), :], 0.0), axis=0, keepdims=True)

    outs = [masses_out]
    for b in range(2):
        lanes = slice(256 * b, 256 * (b + 1))
        product(core * 4 + 2 * b, own.at[b])
        partial_in[b].wait_recv()

        def finish(m, carry):
            rows = pl.ds(pl.multiple_of(m * 64, 64), 64)
            fresh[rows, lanes] = own[b, rows, :] + nrecv[b, rows, :] + PRIOR * cent_ref[rows, lanes]
            return carry

        lax.fori_loop(0, CENTS // 64, finish, 0)
        out = pltpu.make_async_copy(fresh.at[:, lanes], out_ref.at[:, lanes], ls.at[2 + b])
        out.start()
        outs.append(out)

    for out in outs:
        out.wait()
    for copy in pending + partial_in + [mass_in]:
        copy.wait_send()


def divide(total_ref, spread_ref, mass_ref, out_ref, mass_out):
    scale = 1.0 / (spread_ref[...] + PRIOR)
    mass_out[...] = mass_ref[...]
    out_ref[...] = total_ref[...] * jnp.concatenate([scale] * (HALF // LANES), axis=1)


def per_device(points, centroids):
    vmem = pl.BlockSpec(memory_space=pltpu.VMEM)
    hbm = pl.BlockSpec(memory_space=pl.ANY)
    f32, bf16 = jnp.float32, jnp.bfloat16
    total, mass, masses = pl.pallas_call(
        kernel,
        out_shape=(jax.ShapeDtypeStruct((CENTS, HALF), f32), jax.ShapeDtypeStruct((8, LANES), f32),
                   jax.ShapeDtypeStruct((CENTS, LANES), f32)),
        in_specs=[hbm, hbm],
        out_specs=(hbm, vmem, hbm),
        scratch_shapes=[
            pltpu.VMEM((2 * ROWS, HALF), bf16),
            pltpu.VMEM((CENTS, HALF), f32),
            pltpu.VMEM((TILES, NZ, NX, NY, ROWS, LANES), bf16),
            pltpu.VMEM((4, ROWS, LANES), bf16),
            pltpu.VMEM((2, CENTS, HALF), bf16),
            pltpu.VMEM((CENTS, PTS), f32),
            pltpu.VMEM((CENTS, PTS), bf16),
            pltpu.VMEM((CENTS, LANES), f32),
            pltpu.VMEM((CENTS, LANES), f32),
            pltpu.VMEM((CENTS, LANES), f32),
            pltpu.VMEM((PBLOCKS, LANES), f32),
            pltpu.VMEM((ITERS, 8, LANES), f32),
            pltpu.VMEM((ITERS, 8, LANES), f32),
            pltpu.VMEM((ITERS, 2, len(STAGES), 8, LANES), f32),
            pltpu.VMEM((ITERS, 2, STAGE_SEMS - 1, 8, LANES), f32),
            pltpu.VMEM((8, LANES), f32),
            pltpu.VMEM((8, LANES), f32),
            pltpu.VMEM((2, CENTS, 256), f32),
            pltpu.VMEM((2, CENTS, 256), f32),
            pltpu.VMEM((2, CENTS, 256), f32),
            pltpu.VMEM((CENTS, HALF), f32),
            pltpu.SemaphoreType.DMA((GATHER_SEMS,)),
            pltpu.SemaphoreType.DMA((GATHER_SEMS,)),
            pltpu.SemaphoreType.DMA((ITERS, 2, STAGE_SEMS)),
            pltpu.SemaphoreType.DMA((ITERS, 2, STAGE_SEMS)),
            pltpu.SemaphoreType.DMA((3,)),
            pltpu.SemaphoreType.DMA((3,)),
            pltpu.SemaphoreType.DMA((5,)),
        ],
        compiler_params=pltpu.CompilerParams(
            collective_id=0, has_side_effects=True, vmem_limit_bytes=60 * 1024 * 1024),
    )(points, centroids)
    centers, mass = pl.pallas_call(
        divide,
        out_shape=(jax.ShapeDtypeStruct((CENTS, HALF), f32), jax.ShapeDtypeStruct((8, LANES), f32)),
        grid=(CENTS // BLOCK,),
        in_specs=[pl.BlockSpec((BLOCK, HALF), lambda i: (i, 0)), pl.BlockSpec((BLOCK, LANES), lambda i: (i, 0)),
                  pl.BlockSpec((8, LANES), lambda i: (0, 0))],
        out_specs=(pl.BlockSpec((BLOCK, HALF), lambda i: (i, 0)), pl.BlockSpec((8, LANES), lambda i: (0, 0))),
    )(total, masses, mass)
    return centers, mass.reshape(CENTS)


def solution(mesh):
    return jax.shard_map(
        per_device,
        mesh=mesh,
        in_specs=(P("blk", "rep"), P("blk", "rep")),
        out_specs=(P("blk", "rep"), P("blk")),
        check_vma=False,
    )
```
